256 devices in a mesh: rowa: 8 (over x, core), rowb: 32 (over y, z).
Axes of the slice: x: 4, y: 4, z: 8, core: 2. Of those that a mesh axis runs over, the one named last changes fastest.
Arguments:
- embeddings: bfloat16 [262144, 4096], P(('rowa', 'rowb')), may hold values from -250 to 250
- sketch: bfloat16 [4096, 128], replicated, may hold values from -1 to 1
Outputs:
- basis: float32 [262144, 128], P(('rowa', 'rowb'))
- panel_t: float32 [4096, 128], P(('rowa', 'rowb'))
The draws below stay inside these ranges and needn't reach their ends.
All inputs are finite; a program needn't handle non-finite values.
Results may differ from the reference program's by a relative error of at most 0.0046.
Values may be sent and summed in bfloat16 or wider, within the bound.
A program may use at most 64 MiB of HBM per device.

```python
import math
import jax
import jax.numpy as jnp
from jax import lax

D = 4096
K = 128
ROWS = 262144


def draw_embeddings(key, part):
    key = jax.random.fold_in(key, 11)
    keys = jax.random.split(key, 4)
    col_scale = jnp.exp(jax.random.uniform(keys[0], (16, D), jnp.float32, 0.0, math.log(10.0)))
    segment = jnp.arange(ROWS, dtype=jnp.int32) * 16 // ROWS
    row_cols = col_scale[segment]
    col_off = jax.random.uniform(keys[1], (1, D), jnp.float32, -1.5, 1.5)
    row_scale = 0.3 * jnp.exp(jax.random.uniform(keys[2], (ROWS, 1), jnp.float32, 0.0, math.log(10.0)))
    drift = 0.5 + 2.0 * jnp.arange(ROWS, dtype=jnp.float32)[:, None] / ROWS
    noise = jnp.clip(jax.random.normal(keys[3], (ROWS, D), jnp.float32), -6.0, 6.0)
    values = drift * col_off + row_scale * row_cols * noise
    return values.astype(jnp.bfloat16)


def draw_sketch(key, part):
    key = jax.random.fold_in(key, 23)
    keys = jax.random.split(key, 3)
    loads = jax.random.uniform(keys[0], (1, K), jnp.float32, -2.0, 2.0)
    shared = jnp.clip(jax.random.normal(keys[1], (D, 1), jnp.float32), -6.0, 6.0)
    noise = jnp.clip(jax.random.normal(keys[2], (D, K), jnp.float32), -6.0, 6.0)
    values = (noise + shared * loads) / math.sqrt(D * 7.0 / 3.0)
    return values.astype(jnp.bfloat16)


def setup_inputs(seed: int = 0) -> dict:
    seeds = jax.random.split(jax.random.key(seed), 3)
    embeddings = draw_embeddings(jax.random.fold_in(seeds[2], 71), 0)
    sketch = draw_sketch(jax.random.fold_in(seeds[2], 71), 0)
    return {"embeddings": embeddings, "sketch": sketch}


def orthonormal(sketched):
    gram = lax.dot_general(sketched, sketched, (((0,), (0,)), ((), ())), precision=lax.Precision.HIGHEST)
    lower = jnp.linalg.cholesky(gram)
    return lax.linalg.triangular_solve(lower, sketched, left_side=False, lower=True, transpose_a=True)

def project(embeddings, half, mean):
    weight = lax.optimization_barrier(jnp.sum(half.astype(jnp.float32), axis=0))
    prod = jnp.dot(half.T.astype(jnp.float32), embeddings.astype(jnp.float32), preferred_element_type=jnp.float32).T
    return prod - mean[:, None] * weight[None, :]

def reference(embeddings, sketch):
    total_rows = embeddings.shape[0]
    mean = lax.optimization_barrier(jnp.sum(embeddings, axis=0, dtype=jnp.float32)) / total_rows
    center = jnp.dot(mean[None, :], sketch.astype(jnp.float32), precision=lax.Precision.HIGHEST)
    sketched = jnp.dot(embeddings.astype(jnp.float32), sketch.astype(jnp.float32), preferred_element_type=jnp.float32) - center
    first_basis = orthonormal(sketched)
    first_half = first_basis.astype(jnp.bfloat16)
    panel = project(embeddings, first_half, mean)
    panel_half = panel.astype(jnp.bfloat16)
    center_two = jnp.dot(mean[None, :], panel_half.astype(jnp.float32), precision=lax.Precision.HIGHEST)
    second = jnp.dot(embeddings.astype(jnp.float32), panel_half.astype(jnp.float32), preferred_element_type=jnp.float32) - center_two
    second_basis = orthonormal(second)
    root = jnp.sqrt(jnp.float32(total_rows))
    basis = second_basis * root
    second_half = second_basis.astype(jnp.bfloat16)
    panel_t = project(embeddings, second_half, mean) / root
    return (basis, panel_t)
```

```python
import functools

import jax
import jax.numpy as jnp
from jax import lax
from jax.experimental import pallas as pl
from jax.experimental.pallas import tpu as pltpu
from jax.sharding import PartitionSpec as P

F32 = jnp.float32
BF16 = jnp.bfloat16
HIGH = lax.Precision.HIGHEST
K = 128
RING = 4
CHUNKS = 4
BLOCK = 16
SR_ROWS = 24


def dot(a, b, dims, precision=None):
    return lax.dot_general(a, b, (dims, ((), ())), precision=precision, preferred_element_type=F32)


def split(value):
    hi = value.astype(BF16)
    return hi, (value - hi.astype(F32)).astype(BF16)


def rows_tile(row):
    return jnp.broadcast_to(row, (8, row.shape[-1]))


class Net:
    def __init__(self, send_sem, recv_sem):
        self.send_sem, self.recv_sem = send_sem, recv_sem
        self.count = 0
        self.unsent = []

    def send(self, src, dst, device):
        copy = pltpu.make_async_remote_copy(
            src_ref=src,
            dst_ref=dst,
            send_sem=self.send_sem.at[self.count],
            recv_sem=self.recv_sem.at[self.count],
            device_id=device,
            device_id_type=pl.DeviceIdType.MESH,
        )
        self.count += 1
        copy.start()
        self.unsent.append(copy)
        return copy

    def drain(self):
        for copy in self.unsent:
            copy.wait_send()
        self.unsent = []


def inverse_factor(work, out):
    sub = lax.broadcasted_iota(jnp.int32, (BLOCK, K), 0)

    def step(b, carry):
        at = pl.multiple_of(b * BLOCK, BLOCK)
        gram = work[pl.ds(at, BLOCK), :K]
        inv = work[pl.ds(at, BLOCK), K:]
        turned = pltpu.roll(gram, lax.rem(K - at, K), 1)
        cols = [jnp.broadcast_to(turned[:, l : l + 1], (BLOCK, K)) for l in range(BLOCK)]
        pivots = jnp.ones((BLOCK, K), F32)
        for k in range(BLOCK):
            pivot = cols[k][k : k + 1, :]
            pivots = jnp.where(sub == k, pivot, pivots)
            mult = jnp.where(sub > k, cols[k] * (1.0 / pivot), 0.0)
            for l in range(k + 1, BLOCK):
                cols[l] = cols[l] - mult * cols[l][k : k + 1, :]
            gram = gram - mult * gram[k : k + 1, :]
            inv = inv - mult * inv[k : k + 1, :]
        scale = 1.0 / jnp.sqrt(pivots)
        gram = gram * scale
        inv = inv * scale
        out[pl.ds(at, BLOCK), :] = inv
        both = jnp.concatenate([gram, inv], axis=1)
        work[...] = work[...] - dot(gram, both, ((0,), (0,)), HIGH)
        return carry

    lax.fori_loop(0, K // BLOCK, step, 0)


def kernel(
    dims, total_rows, emb, sketch, basis, panel_t,
    e_v, om_v, y_v, zt, zc, colsum, buf, part, core_in, ring1, ring2, zsrc, z_in,
    sr, sr_core, sr_x, sr_y, sr_z, gram, work, fac, sa_src, sa_in, ph,
    load_sem, send_sem, recv_sem,
):
    X, Y, Z = dims
    rows = emb.shape[0]
    width = emb.shape[1]
    chunk = rows // CHUNKS
    share = K // Z
    inv_rows = 1.0 / total_rows

    loads = [pltpu.make_async_copy(sketch, om_v, load_sem.at[CHUNKS])]
    for i in range(CHUNKS):
        piece = pl.ds(i * chunk, chunk)
        loads.append(pltpu.make_async_copy(emb.at[piece], e_v.at[piece], load_sem.at[i]))
    for load in loads:
        load.start()

    a, b = lax.axis_index("rowa"), lax.axis_index("rowb")
    x, c = a // 2, a % 2
    y, z = b // Z, b % Z

    def dev(dx=0, dc=0, dy=0, dz=0):
        return (((x + dx) % X) * 2 + (c + dc) % 2, ((y + dy) % Y) * Z + (z + dz) % Z)

    core_peer = [dev(dc=1)]
    x_peers = [dev(dx=k) for k in range(1, X)]
    y_peers = [dev(dy=k) for k in range(1, Y)]
    z_peers = [dev(dz=k) for k in range(1, Z)]
    peers = core_peer + x_peers + y_peers + z_peers
    barrier = pltpu.get_barrier_semaphore()
    for peer in peers:
        pl.semaphore_signal(barrier, inc=1, device_id=peer, device_id_type=pl.DeviceIdType.MESH)

    net = Net(send_sem, recv_sem)
    groups = ((x, x_peers), (y, y_peers))

    def small_send(use, stage, who, value):
        first = (0, 1, X, X + Y - 1)[stage]
        sa_src[use, stage] = value
        return [
            net.send(sa_src.at[use, stage], sa_in.at[use, first + k], peer) for k, peer in enumerate(who)
        ]

    def small_recv(use, stage, copies):
        first = (0, 1, X, X + Y - 1)[stage]
        value = sa_src[use, stage]
        for k, copy in enumerate(copies):
            copy.wait_recv()
            value = value + sa_in[use, first + k]
        return value

    def sketch_chunk(i):
        loads[i + 1].wait()
        piece = pl.ds(i * chunk, chunk)
        y_v[piece, :] = dot(e_v[piece, :], om_v[...], ((1,), (0,)))
        block = e_v[piece, :].astype(F32)
        partial = jnp.sum(block.reshape(chunk // 8, 8, width), axis=0)
        colsum[...] = partial if i == 0 else colsum[...] + partial

    loads[0].wait()
    sketch_chunk(0)
    sample = jnp.sum(y_v[pl.ds(0, chunk), :], axis=0, keepdims=True) * (1.0 / chunk)
    pl.semaphore_wait(barrier, len(peers))
    flight = small_send(0, 0, core_peer, rows_tile(sample))
    sketch_chunk(1)
    flight = small_send(0, 1, x_peers, small_recv(0, 0, flight))
    sketch_chunk(2)
    flight = small_send(0, 2, y_peers, small_recv(0, 1, flight))
    sketch_chunk(3)
    flight = small_send(0, 3, z_peers, small_recv(0, 2, flight))
    shift = small_recv(0, 3, flight)[:1] * (1.0 / (2 * X * Y * Z))

    def small_record(value, sums):
        hi, lo = split(value)
        zc[:, :K] = hi
        zc[:, K:] = lo
        zt[...] = zc[...].T
        w = jnp.sum(hi.astype(F32) + lo.astype(F32), axis=0, keepdims=True)
        four = dot(zt[...], zc[...], ((1,), (0,)))
        full = (four[:K, :K] + four[K:, K:]) + (four[:K, K:] + four[K:, :K])
        for cc in range(2):
            for xx in range(X):
                sr[cc, xx, 0:16] = full[(cc * X + xx) * 16 : (cc * X + xx + 1) * 16]
                for yy in range(Y):
                    j = (xx * 2 + cc) * Y + yy
                    sr[cc, xx, 16 + yy : 17 + yy] = sums[:, j * K : (j + 1) * K]
                sr[cc, xx, 16 + Y : 24] = jnp.broadcast_to(w, (8 - Y, K))

    def products(core, into):
        def step(xx, carry):
            for yp in range(0, Y, 2):
                at = pl.multiple_of(((xx * 2 + core) * Y + yp) * K, 2 * K)
                prod = dot(zt[...], e_v[:, pl.ds(at, 2 * K)], ((1,), (0,)))
                prod = prod[:K] + prod[K:]
                for k in range(2):
                    into[0, xx, yp + k] = prod[: K // 2, k * K : (k + 1) * K]
                    into[1, yp + k, xx] = prod[K // 2 :, k * K : (k + 1) * K]
            return carry

        return step

    def reduce(ph_id, value, sums):
        small_record(value, sums)
        core_flight = net.send(sr.at[1 - c], sr_core.at[ph_id], core_peer[0])
        partner = products(1 - c, part)
        panels = []
        for xx in range(X):
            partner(xx, 0)
            panels.append(net.send(part.at[0, xx], core_in.at[ph_id, 0, xx], core_peer[0]))
            panels.append(net.send(part.at[1, :, xx], core_in.at[ph_id, 1, :, xx], core_peer[0]))
        core_flight.wait_recv()
        sr[c] = sr[c] + sr_core[ph_id]
        xf = [
            net.send(sr.at[c, (x + k + 1) % X], sr_x.at[ph_id, k], peer) for k, peer in enumerate(x_peers)
        ]
        lax.fori_loop(0, X, products(c, buf), 0)

        record = sr[c, x]
        for k, copy in enumerate(xf):
            copy.wait_recv()
            record = record + sr_x[ph_id, k]
        sr_y[ph_id, Y - 1] = record
        yf = [net.send(sr_y.at[ph_id, Y - 1], sr_y.at[ph_id, k], peer) for k, peer in enumerate(y_peers)]

        for copy in panels:
            copy.wait_recv()
        for g in range(2):
            for t in range(RING):
                buf[g, t] = buf[g, t] + core_in[ph_id, g, t]

        def ring_start(views, land):
            sent = []
            for g in range(2):
                me, who = views[g][0], views[g][1]
                piece = views[g][2]
                nxt, prv = who[0], who[RING - 2]
                far, fwd, back = (me + 2) % RING, (me + 1) % RING, (me + 3) % RING
                sent.append([
                    net.send(piece(far, 0), land.at[ph_id, g, 0], nxt),
                    net.send(piece(far, 1), land.at[ph_id, g, 1], prv),
                    net.send(piece(fwd, 1), land.at[ph_id, g, 2], nxt),
                    net.send(piece(back, 0), land.at[ph_id, g, 3], prv),
                ])
            return sent

        def ring_relay(views, land, sent):
            for g in range(2):
                me, who, piece = views[g]
                nxt, prv = who[0], who[RING - 2]
                fwd, back = (me + 1) % RING, (me + 3) % RING
                sent[g][0].wait_recv()
                ref = piece(fwd, 0)
                ref[...] = ref[...] + land[ph_id, g, 0]
                sent[g].append(net.send(ref, land.at[ph_id, g, 4], nxt))
                sent[g][1].wait_recv()
                ref = piece(back, 1)
                ref[...] = ref[...] + land[ph_id, g, 1]
                sent[g].append(net.send(ref, land.at[ph_id, g, 5], prv))

        def ring_finish(views, land, sent):
            for g in range(2):
                me, _, piece = views[g]
                for copy in sent[g][2:]:
                    copy.wait_recv()
                ref = piece(me, 0)
                ref[...] = ref[...] + land[ph_id, g, 4] + land[ph_id, g, 3]
                ref = piece(me, 1)
                ref[...] = ref[...] + land[ph_id, g, 2] + land[ph_id, g, 5]

        half = RING // 2
        quarter = K // 4

        def outer(g):
            return lambda t, h: buf.at[g, t, pl.ds(h * half, half)]

        def inner(g, me):
            return lambda t, h: buf.at[g, me, t, pl.ds(h * quarter, quarter)]

        views1 = [(groups[g][0], groups[g][1], outer(g)) for g in range(2)]
        views2 = [(groups[1 - g][0], groups[1 - g][1], inner(g, groups[g][0])) for g in range(2)]

        sent = ring_start(views1, ring1)

        record = sr_y[ph_id, Y - 1]
        for k, copy in enumerate(yf):
            copy.wait_recv()
            record = record + sr_y[ph_id, k]
        sr_z[ph_id, Z - 1] = record
        zf = [net.send(sr_z.at[ph_id, Z - 1], sr_z.at[ph_id, k], peer) for k, peer in enumerate(z_peers)]

        ring_relay(views1, ring1, sent)

        record = sr_z[ph_id, Z - 1]
        for k, copy in enumerate(zf):
            copy.wait_recv()
            record = record + sr_z[ph_id, k]
        rest = record[16:]
        mine = pl.ds(pl.multiple_of((c * X + x) * 16, 16), 16)
        gram[ph_id, mine, :] = record[:16]
        gf = [net.send(gram.at[ph_id, mine], gram.at[ph_id, mine], peer) for peer in x_peers]

        ring_finish(views1, ring1, sent)
        sent = ring_start(views2, ring2)

        for copy in gf:
            copy.wait_recv()
        mine = pl.ds(pl.multiple_of(c * 64, 64), 64)
        last = net.send(gram.at[ph_id, mine], gram.at[ph_id, mine], core_peer[0])

        ring_relay(views2, ring2, sent)
        ring_finish(views2, ring2, sent)

        zsrc[:, : K // 2] = buf[0, x, y].T
        zsrc[:, K // 2 :] = buf[1, y, x].T
        pf = [
            net.send(
                zsrc.at[pl.ds(pl.multiple_of(((z + k + 1) % Z) * share, share), share)],
                z_in.at[ph_id, k],
                peer,
            )
            for k, peer in enumerate(z_peers)
        ]
        last.wait_recv()
        w = rest[Y : Y + 1]
        wt = rows_tile(w)
        work[:, :K] = gram[ph_id] - dot(wt, wt, ((0,), (0,)), HIGH) * (inv_rows / 8)
        eye = lax.broadcasted_iota(jnp.int32, (K, K), 0) == lax.broadcasted_iota(jnp.int32, (K, K), 1)
        work[:, K:] = eye.astype(F32)
        inverse_factor(work, fac)
        mine = zsrc[pl.ds(pl.multiple_of(z * share, share), share), :]
        for k, copy in enumerate(pf):
            copy.wait_recv()
            mine = mine + z_in[ph_id, k]
        net.drain()
        return mine, w, rest

    sums = jnp.sum(colsum[...], axis=0, keepdims=True)
    mine, w, rest = reduce(0, y_v[...] - shift, sums)
    sub = lax.broadcasted_iota(jnp.int32, (8, K), 0)
    own = jnp.sum(jnp.where(sub == y, rest, 0.0), axis=0, keepdims=True)
    lane = lax.broadcasted_iota(jnp.int32, (share, K), 1)
    row = lax.broadcasted_iota(jnp.int32, (share, K), 0)
    mean = jnp.sum(jnp.where(lane == row + z * share, own, 0.0), axis=1, keepdims=True) * inv_rows
    panel = dot(mine - mean * w, fac[...], ((1,), (1,)), HIGH).astype(BF16)
    place = pl.ds(pl.multiple_of(z * share, share), share)
    ph[x, c, y, place, :] = panel
    flight = [net.send(ph.at[x, c, y, place], ph.at[x, c, y, place], peer) for peer in z_peers]
    center = jnp.sum(mean * panel.astype(F32), axis=0, keepdims=True)
    small = small_send(1, 3, z_peers, rows_tile(center))
    for copy in flight:
        copy.wait_recv()

    def gather_start(views):
        sent = []
        for me, who, piece in views:
            own_piece = piece(me)
            sent.append([net.send(own_piece, own_piece, who[0]), net.send(own_piece, own_piece, who[RING - 2])])
        return sent

    def gather_relay(views, sent):
        for g, (me, who, piece) in enumerate(views):
            sent[g][0].wait_recv()
            ref = piece((me + 3) % RING, 0)
            relay = [net.send(ref, ref, who[0])]
            sent[g][1].wait_recv()
            ref = piece((me + 1) % RING, 1)
            relay.append(net.send(ref, ref, who[RING - 2]))
            sent[g].extend(relay)

    def gather_finish(sent):
        for copies in sent:
            for copy in copies[2:]:
                copy.wait_recv()

    low, high = pl.ds(0, K // 2), pl.ds(K // 2, K // 2)

    def first_piece(g):
        def piece(t, h=None):
            start = g * (K // 2) + (0 if h is None else h * (K // 4))
            part_rows = pl.ds(start, K // 2 if h is None else K // 4)
            return ph.at[x, c, t, part_rows] if g == 0 else ph.at[t, c, y, part_rows]

        return piece

    def second_piece(g):
        def piece(t, h=None):
            span = pl.ds(0, RING) if h is None else pl.ds(h * (RING // 2), RING // 2)
            return ph.at[t, c, span, low] if g == 0 else ph.at[span, c, t, high]

        return piece

    views1 = [(groups[1 - g][0], groups[1 - g][1], first_piece(g)) for g in range(2)]
    views2 = [(groups[g][0], groups[g][1], second_piece(g)) for g in range(2)]
    sent = gather_start(views1)
    small = small_send(1, 2, y_peers, small_recv(1, 3, small))
    gather_relay(views1, sent)
    gather_finish(sent)
    sent = gather_start(views2)
    small = small_send(1, 1, x_peers, small_recv(1, 2, small))
    gather_relay(views2, sent)
    small = small_send(1, 0, core_peer, small_recv(1, 1, small))
    gather_finish(sent)
    last = [net.send(ph.at[xx, c], ph.at[xx, c], core_peer[0]) for xx in range(X)]

    def second(core, xx):
        at = pl.multiple_of((xx * 2 + core) * Y * K, Y * K)
        right = ph[xx, core].reshape(Y * K, K)
        y_v[...] = y_v[...] + dot(e_v[:, pl.ds(at, Y * K)], right, ((1,), (0,)))

    center = small_recv(1, 0, small)[:1]
    y_v[...] = jnp.broadcast_to(-center, (rows, K))
    for xx in range(X):
        second(c, xx)
    for xx in range(X):
        last[xx].wait_recv()
        second(1 - c, xx)
    net.drain()

    mine, w, _ = reduce(1, y_v[...], jnp.zeros((1, width), F32))
    root = jnp.sqrt(jnp.full((1, K), total_rows, F32))
    basis[...] = dot(y_v[...] - w * inv_rows, fac[...], ((1,), (1,)), HIGH) * root
    panel_t[...] = dot(mine - mean * w, fac[...], ((1,), (1,)), HIGH) / root
    net.drain()


def on_device(dims, embeddings, sketch):
    X, Y, Z = dims
    rows, width = embeddings.shape
    total_rows = rows * X * 2 * Y * Z
    share = K // Z
    vm = pltpu.VMEM
    transfers = 8 + 2 * (1 + 8 + 2 * (X + Y + Z) + 24 + Z) + 2 * (X + Y + Z) + Z + 16 + X
    return pl.pallas_call(
        functools.partial(kernel, dims, float(total_rows)),
        out_shape=(
            jax.ShapeDtypeStruct((rows, K), F32),
            jax.ShapeDtypeStruct((share, K), F32),
        ),
        in_specs=[pl.BlockSpec(memory_space=pl.ANY)] * 2,
        out_specs=(pl.BlockSpec(memory_space=vm), pl.BlockSpec(memory_space=vm)),
        scratch_shapes=[
            vm((rows, width), BF16),
            vm((width, K), BF16),
            vm((rows, K), F32),
            vm((2 * K, rows), BF16),
            vm((rows, 2 * K), BF16),
            vm((8, width), F32),
            vm((2, RING, RING, K // 2, K), F32),
            vm((2, RING, RING, K // 2, K), F32),
            vm((2, 2, RING, RING, K // 2, K), F32),
            vm((2, 2, 6, RING // 2, K // 2, K), F32),
            vm((2, 2, 6, K // 4, K), F32),
            vm((K, K), F32),
            vm((2, Z - 1, share, K), F32),
            vm((2, X, SR_ROWS, K), F32),
            vm((2, X, SR_ROWS, K), F32),
            vm((2, X - 1, SR_ROWS, K), F32),
            vm((2, Y, SR_ROWS, K), F32),
            vm((2, Z, SR_ROWS, K), F32),
            vm((2, K, K), F32),
            vm((K, 2 * K), F32),
            vm((K, K), F32),
            vm((2, 4, 8, K), F32),
            vm((2, X + Y + Z - 2, 8, K), F32),
            vm((X, 2, Y, K, K), BF16),
            pltpu.SemaphoreType.DMA((CHUNKS + 1,)),
            pltpu.SemaphoreType.DMA((transfers,)),
            pltpu.SemaphoreType.DMA((transfers,)),
        ],
        compiler_params=pltpu.CompilerParams(
            collective_id=0, has_side_effects=True, vmem_limit_bytes=56 * 1024 * 1024
        ),
        name="pca",
    )(embeddings, sketch)


def solution(mesh):
    X, Y = mesh.shape["rowa"] // 2, 4
    dims = (X, Y, mesh.shape["rowb"] // Y)
    spread = P(("rowa", "rowb"), None)
    return jax.shard_map(
        functools.partial(on_device, dims),
        mesh=mesh,
        in_specs=(spread, P()),
        out_specs=(spread, spread),
        check_vma=False,
    )
```

```python
import functools

import jax
import jax.numpy as jnp
from jax import lax
from jax.experimental import pallas as pl
from jax.experimental.pallas import tpu as pltpu
from jax.sharding import PartitionSpec as P

F32 = jnp.float32
BF16 = jnp.bfloat16
HIGH = lax.Precision.HIGHEST
K = 128
RING = 4
CHUNKS = 4
BLOCK = 16


def dot(a, b, dims, precision=None):
    return lax.dot_general(a, b, (dims, ((), ())), precision=precision, preferred_element_type=F32)


def split(value):
    hi = value.astype(BF16)
    return hi, (value - hi.astype(F32)).astype(BF16)


class Net:
    def __init__(self, send_sem, recv_sem):
        self.send_sem, self.recv_sem = send_sem, recv_sem
        self.count = 0
        self.unsent = []

    def send(self, src, dst, device):
        copy = pltpu.make_async_remote_copy(
            src_ref=src,
            dst_ref=dst,
            send_sem=self.send_sem.at[self.count],
            recv_sem=self.recv_sem.at[self.count],
            device_id=device,
            device_id_type=pl.DeviceIdType.MESH,
        )
        self.count += 1
        copy.start()
        self.unsent.append(copy)
        return copy

    def drain(self):
        for copy in self.unsent:
            copy.wait_send()
        self.unsent = []


def inverse_factor(work, out):
    sub = lax.broadcasted_iota(jnp.int32, (BLOCK, K), 0)

    def step(b, carry):
        at = pl.multiple_of(b * BLOCK, BLOCK)
        gram = work[pl.ds(at, BLOCK), :K]
        inv = work[pl.ds(at, BLOCK), K:]
        turned = pltpu.roll(gram, lax.rem(K - at, K), 1)
        cols = [jnp.broadcast_to(turned[:, l : l + 1], (BLOCK, K)) for l in range(BLOCK)]
        pivots = jnp.ones((BLOCK, K), F32)
        for k in range(BLOCK):
            pivot = cols[k][k : k + 1, :]
            pivots = jnp.where(sub == k, pivot, pivots)
            mult = jnp.where(sub > k, cols[k] * (1.0 / pivot), 0.0)
            for l in range(k + 1, BLOCK):
                cols[l] = cols[l] - mult * cols[l][k : k + 1, :]
            gram = gram - mult * gram[k : k + 1, :]
            inv = inv - mult * inv[k : k + 1, :]
        scale = 1.0 / jnp.sqrt(pivots)
        gram = gram * scale
        inv = inv * scale
        out[pl.ds(at, BLOCK), :] = inv
        both = jnp.concatenate([gram, inv], axis=1)
        work[...] = work[...] - dot(gram, both, ((0,), (0,)), HIGH)
        return carry

    lax.fori_loop(0, K // BLOCK, step, 0)


def kernel(
    dims, emb, sketch, basis, panel_t,
    e_v, om_v, y_v, zt, zc, colsum, buf, part, core_in, land1, land2, zsrc, z_in,
    sr, sr_core, sr_x, y_src, sr_y, z_rec, sr_z, m3c, mzc, corr, gram, work, fac, ph,
    load_sem, send_sem, recv_sem,
):
    X, Y, Z = dims
    rows = emb.shape[0]
    width = emb.shape[1]
    chunk = rows // CHUNKS
    share = K // Z

    loads = [pltpu.make_async_copy(sketch, om_v, load_sem.at[CHUNKS])]
    for i in range(CHUNKS):
        piece = pl.ds(i * chunk, chunk)
        loads.append(pltpu.make_async_copy(emb.at[piece], e_v.at[piece], load_sem.at[i]))
    for load in loads:
        load.start()

    a, b = lax.axis_index("rowa"), lax.axis_index("rowb")
    x, c = a // 2, a % 2
    y, z = b // Z, b % Z

    def dev(dx=0, dc=0, dy=0, dz=0):
        return (((x + dx) % X) * 2 + (c + dc) % 2, ((y + dy) % Y) * Z + (z + dz) % Z)

    core_peer = dev(dc=1)
    x_peers = [dev(dx=k) for k in range(1, X)]
    y_peers = [dev(dy=k) for k in range(1, Y)]
    z_peers = [dev(dz=k) for k in range(1, Z)]
    peers = [core_peer] + x_peers + y_peers + z_peers
    barrier = pltpu.get_barrier_semaphore()
    for peer in peers:
        pl.semaphore_signal(barrier, inc=1, device_id=peer, device_id_type=pl.DeviceIdType.MESH)

    net = Net(send_sem, recv_sem)
    sub = lax.broadcasted_iota(jnp.int32, (8, K), 0)

    def group_mean(tile_rows, count):
        return jnp.sum(tile_rows, axis=0, keepdims=True) * (1.0 / count)

    def outer(left, right):
        return dot(left, right, ((0,), (0,)), HIGH)

    loads[0].wait()
    for i in range(CHUNKS):
        loads[i + 1].wait()
        piece = pl.ds(i * chunk, chunk)
        y_v[piece, :] = dot(e_v[piece, :], om_v[...], ((1,), (0,)))
        block = e_v[piece, :].astype(F32)
        partial = jnp.sum(block.reshape(chunk // 8, 8, width), axis=0)
        colsum[...] = partial if i == 0 else colsum[...] + partial

    def center():
        first = jnp.sum(y_v[...], axis=0, keepdims=True) * (1.0 / rows)
        value = y_v[...] - first
        rest = jnp.sum(value, axis=0, keepdims=True) * (1.0 / rows)
        y_v[...] = value - rest
        return first + rest

    def products(core, xx, add):
        for yp in range(0, Y, 2):
            at = pl.multiple_of(((xx * 2 + core) * Y + yp) * K, 2 * K)
            prod = dot(zt[...], e_v[:, pl.ds(at, 2 * K)], ((1,), (0,)))
            prod = prod[:K] + prod[K:]
            for k in range(2):
                top = prod[: K // 2, k * K : (k + 1) * K]
                low = prod[K // 2 :, k * K : (k + 1) * K]
                if add is None:
                    part[0, xx, yp + k] = top
                    part[1, yp + k, xx] = low
                else:
                    buf[0, xx, yp + k] = top + core_in[add, 0, xx, yp + k]
                    buf[1, yp + k, xx] = low + core_in[add, 1, yp + k, xx]

    def reduce(p, local_mean):
        shift = center()
        hi, lo = split(y_v[...])
        zc[:, :K] = hi
        zc[:, K:] = lo
        zt[...] = zc[...].T
        four = dot(zt[...], zc[...], ((1,), (0,)))
        full = (four[:K, :K] + four[K:, K:]) + (four[:K, K:] + four[K:, :K])
        count = 24 if local_mean is None else 24 + 8 * Y
        for cc in range(2):
            for xx in range(X):
                sr[cc, xx, 0:16] = full[(cc * X + xx) * 16 : (cc * X + xx + 1) * 16]
                sr[cc, xx, 16:24] = jnp.where(sub == a, shift, 0.0)
                if local_mean is not None:
                    for yy in range(Y):
                        j = (xx * 2 + cc) * Y + yy
                        tile = jnp.where(sub == a, local_mean[:, j * K : (j + 1) * K], 0.0)
                        sr[cc, xx, 24 + 8 * yy : 32 + 8 * yy] = tile
        if p == 0:
            pl.semaphore_wait(barrier, len(peers))
        sent_rows = pl.ds(0, count)
        core_flight = net.send(sr.at[1 - c, :, sent_rows], sr_core.at[p, :, sent_rows], core_peer)

        order = [(x + k) % X for k in (2, 1, 3, 0)]
        panels = []
        for xx in order:
            products(1 - c, xx, None)
            panels.append((
                net.send(part.at[0, xx], core_in.at[p, 0, xx], core_peer),
                net.send(part.at[1, :, xx], core_in.at[p, 1, :, xx], core_peer),
            ))
        core_flight.wait_recv()
        sr[c, :, sent_rows] = sr[c, :, sent_rows] + sr_core[p, :, sent_rows]
        xf = [
            net.send(sr.at[c, (x + k + 1) % X, sent_rows], sr_x.at[p, k, sent_rows], peer)
            for k, peer in enumerate(x_peers)
        ]
        first_a = []
        for k, xx in zip((2, 1, 3, 0), order):
            for copy in panels.pop(0):
                copy.wait_recv()
            products(c, xx, p)
            if k:
                first_a.append(net.send(buf.at[0, xx], land1.at[p, 0, k - 1], x_peers[k - 1]))
        first_b = [
            net.send(buf.at[1, (y + k) % Y], land1.at[p, 1, k - 1], y_peers[k - 1]) for k in (2, 1, 3)
        ]

        record = sr[c, x, sent_rows]
        for k, copy in enumerate(xf):
            copy.wait_recv()
            record = record + sr_x[p, k, sent_rows]
        y_src[p, sent_rows] = record
        yf = []
        head = pl.ds(0, 24)
        for k, peer in enumerate(y_peers):
            yf.append(net.send(y_src.at[p, head], sr_y.at[p, k, head], peer))
            if local_mean is not None:
                tile = pl.ds(pl.multiple_of(24 + 8 * ((y + k + 1) % Y), 8), 8)
                yf.append(net.send(y_src.at[p, tile], sr_y.at[p, k, pl.ds(24, 8)], peer))
        for copy in yf:
            copy.wait_recv()
        own_gram = y_src[p, 0:16]
        shifts = [y_src[p, 16:24]]
        for k in range(Y - 1):
            own_gram = own_gram + sr_y[p, k, 0:16]
            shifts.append(sr_y[p, k, 16:24])
        shifts = jnp.concatenate(shifts, axis=0)
        group_shift = group_mean(shifts, 8 * Y)
        shifts = shifts - group_shift
        if local_mean is not None:
            means = [y_src[p, pl.ds(pl.multiple_of(24 + 8 * y, 8), 8)]]
            means += [sr_y[p, k, 24:32] for k in range(Y - 1)]
            means = jnp.concatenate(means, axis=0)
            group = group_mean(means, 8 * Y)
            m3c[...] = means - group
        else:
            group = group_shift
        place = pl.ds(pl.multiple_of((c * X + x) * 16, 16), 16)
        corr[0] = outer(shifts, shifts) * rows
        z_rec[p, 0:16] = own_gram + corr[0, place, :]
        z_rec[p, 16:24] = jnp.where(sub == 0, group, jnp.where(sub == 1, group_shift, 0.0))
        zf = [net.send(z_rec.at[p], sr_z.at[p, k], peer) for k, peer in enumerate(z_peers)]
        corr[1] = outer(m3c[...], shifts) * rows

        def collect(g, at, copies, land):
            ref = buf.at[g, at[0]] if len(at) == 1 else buf.at[g, at[0], at[1]]
            total = ref[...]
            for copy in copies:
                copy.wait_recv()
            for k in range(RING - 1):
                total = total + land[p, g, k]
            ref[...] = total

        collect(0, (x,), first_a, land1)
        second_a = [
            net.send(buf.at[0, x, (y + k) % Y], land2.at[p, 0, k - 1], y_peers[k - 1]) for k in (2, 1, 3)
        ]
        collect(1, (y,), first_b, land1)
        second_b = [
            net.send(buf.at[1, y, (x + k) % X], land2.at[p, 1, k - 1], x_peers[k - 1]) for k in (2, 1, 3)
        ]

        total = z_rec[p, 0:16]
        tiles = [z_rec[p, 16:24]]
        for k, copy in enumerate(zf):
            copy.wait_recv()
            total = total + sr_z[p, k, 0:16]
            tiles.append(sr_z[p, k, 16:24])
        gram[p, place, :] = total
        gf = [net.send(gram.at[p, place], gram.at[p, place], peer) for peer in x_peers]
        mz = jnp.zeros((8, K), F32)
        sz = jnp.zeros((8, K), F32)
        for k, tile in enumerate(tiles):
            mz = jnp.where(sub == k, tile[0:1], mz)
            sz = jnp.where(sub == k, tile[1:2], sz)
        mean_shift = group_mean(sz, Z)
        sz = jnp.where(sub < Z, sz - mean_shift, 0.0)
        if local_mean is not None:
            mzc[...] = jnp.where(sub < Z, mz - group_mean(mz, Z), 0.0)
        weight = float(rows * 2 * X * Y)
        corr[2] = outer(mzc[...], sz) * weight
        corr[0] = outer(sz, sz) * weight

        collect(0, (x, y), second_a, land2)
        collect(1, (y, x), second_b, land2)
        zsrc[:, : K // 2] = buf[0, x, y].T + corr[1, :, : K // 2]
        zsrc[:, K // 2 :] = buf[1, y, x].T + corr[1, :, K // 2 :]
        pf = [
            net.send(
                zsrc.at[pl.ds(pl.multiple_of(((z + k + 1) % Z) * share, share), share)],
                z_in.at[p, k],
                peer,
            )
            for k, peer in enumerate(z_peers)
        ]
        for copy in gf:
            copy.wait_recv()
        place = pl.ds(pl.multiple_of(c * (K // 2), K // 2), K // 2)
        last = net.send(gram.at[p, place], gram.at[p, place], core_peer)
        eye = lax.broadcasted_iota(jnp.int32, (K, K), 0) == lax.broadcasted_iota(jnp.int32, (K, K), 1)
        work[:, K:] = eye.astype(F32)
        last.wait_recv()
        work[:, :K] = gram[p] + corr[0]
        inverse_factor(work, fac)
        place = pl.ds(pl.multiple_of(z * share, share), share)
        mine = zsrc[place, :] + corr[2, place, :]
        for k, copy in enumerate(pf):
            copy.wait_recv()
            mine = mine + z_in[p, k]
        net.drain()
        return mine, shift - mean_shift

    local_mean = jnp.sum(colsum[...], axis=0, keepdims=True) * (1.0 / rows)
    mine, _ = reduce(0, local_mean)
    panel = dot(mine, fac[...], ((1,), (1,)), HIGH).astype(BF16)
    place = pl.ds(pl.multiple_of(z * share, share), share)
    ph[x, c, y, place, :] = panel
    flight = [net.send(ph.at[x, c, y, place], ph.at[x, c, y, place], peer) for peer in z_peers]
    for copy in flight:
        copy.wait_recv()
    low, high = pl.ds(0, K // 2), pl.ds(K // 2, K // 2)
    near, far = ph.at[x, c, y, low], ph.at[x, c, y, high]
    flight_a = [net.send(near, near, y_peers[k - 1]) for k in (2, 1, 3)]
    flight_b = [net.send(far, far, x_peers[k - 1]) for k in (2, 1, 3)]
    for copy in flight_a:
        copy.wait_recv()
    near, far = ph.at[x, c, :, low], ph.at[:, c, y, high]
    flight_a = [net.send(near, near, x_peers[k - 1]) for k in (2, 1, 3)]
    for copy in flight_b:
        copy.wait_recv()
    flight_b = [net.send(far, far, y_peers[k - 1]) for k in (2, 1, 3)]
    for copy in flight_a:
        copy.wait_recv()
    near, far = ph.at[:, c, :, low], ph.at[:, c, :, high]
    last = [net.send(near, near, core_peer)]
    for copy in flight_b:
        copy.wait_recv()
    last.append(net.send(far, far, core_peer))

    def second(core, xx):
        at = pl.multiple_of((xx * 2 + core) * Y * K, Y * K)
        right = ph[xx, core].reshape(Y * K, K)
        return dot(e_v[:, pl.ds(at, Y * K)], right, ((1,), (0,)))

    y_v[...] = second(c, 0)
    for xx in range(1, X):
        y_v[...] = y_v[...] + second(c, xx)
    for copy in last:
        copy.wait_recv()
    for xx in range(X):
        y_v[...] = y_v[...] + second(1 - c, xx)
    net.drain()

    mine, offset = reduce(1, None)
    root = jnp.sqrt(jnp.full((1, K), rows * 2 * X * Y * Z, F32))
    basis[...] = dot(y_v[...] + offset, fac[...], ((1,), (1,)), HIGH) * root
    panel_t[...] = dot(mine, fac[...], ((1,), (1,)), HIGH) / root


def copy_out(basis_in, panel_in, basis_out, panel_out, sems):
    copies = [
        pltpu.make_async_copy(basis_in, basis_out, sems.at[0]),
        pltpu.make_async_copy(panel_in, panel_out, sems.at[1]),
    ]
    for copy in copies:
        copy.start()
    for copy in copies:
        copy.wait()


def on_device(dims, embeddings, sketch):
    X, Y, Z = dims
    rows, width = embeddings.shape
    share = K // Z
    record = 24 + 8 * Y
    vm = pltpu.VMEM
    transfers = 2 * (18 + 5 * (X + Y) + 2 * Z) + Z + 2 * (X + Y)
    results = pl.pallas_call(
        functools.partial(kernel, dims),
        out_shape=(
            jax.ShapeDtypeStruct((rows, K), F32),
            jax.ShapeDtypeStruct((share, K), F32),
        ),
        in_specs=[pl.BlockSpec(memory_space=pl.ANY)] * 2,
        out_specs=(pl.BlockSpec(memory_space=vm), pl.BlockSpec(memory_space=vm)),
        scratch_shapes=[
            vm((rows, width), BF16),
            vm((width, K), BF16),
            vm((rows, K), F32),
            vm((2 * K, rows), BF16),
            vm((rows, 2 * K), BF16),
            vm((8, width), F32),
            vm((2, RING, RING, K // 2, K), F32),
            vm((2, RING, RING, K // 2, K), F32),
            vm((2, 2, RING, RING, K // 2, K), F32),
            vm((2, 2, RING - 1, RING, K // 2, K), F32),
            vm((2, 2, RING - 1, K // 2, K), F32),
            vm((K, K), F32),
            vm((2, Z - 1, share, K), F32),
            vm((2, X, record, K), F32),
            vm((2, X, record, K), F32),
            vm((2, X - 1, record, K), F32),
            vm((2, record, K), F32),
            vm((2, Y - 1, 32, K), F32),
            vm((2, 24, K), F32),
            vm((2, Z - 1, 24, K), F32),
            vm((8 * Y, K), F32),
            vm((8, K), F32),
            vm((3, K, K), F32),
            vm((2, K, K), F32),
            vm((K, 2 * K), F32),
            vm((K, K), F32),
            vm((X, 2, Y, K, K), BF16),
            pltpu.SemaphoreType.DMA((CHUNKS + 1,)),
            pltpu.SemaphoreType.DMA((transfers,)),
            pltpu.SemaphoreType.DMA((transfers,)),
        ],
        compiler_params=pltpu.CompilerParams(
            collective_id=0, has_side_effects=True, vmem_limit_bytes=56 * 1024 * 1024
        ),
        name="pca",
    )(embeddings, sketch)
    return pl.pallas_call(
        copy_out,
        out_shape=[jax.ShapeDtypeStruct(value.shape, F32) for value in results],
        in_specs=[pl.BlockSpec(memory_space=pl.ANY)] * 2,
        out_specs=[pl.BlockSpec(memory_space=pl.ANY)] * 2,
        scratch_shapes=[pltpu.SemaphoreType.DMA((2,))],
        name="copy_out",
    )(*results)


def solution(mesh):
    X, Y = mesh.shape["rowa"] // 2, 4
    dims = (X, Y, mesh.shape["rowb"] // Y)
    spread = P(("rowa", "rowb"), None)
    return jax.shard_map(
        functools.partial(on_device, dims),
        mesh=mesh,
        in_specs=(spread, P()),
        out_specs=(spread, spread),
        check_vma=False,
    )
```

```python
import functools

import jax
import jax.numpy as jnp
from jax import lax
from jax.experimental import pallas as pl
from jax.experimental.pallas import tpu as pltpu
from jax.sharding import PartitionSpec as P

F32 = jnp.float32
BF16 = jnp.bfloat16
HIGH = lax.Precision.HIGHEST
K = 128
RING = 4
CHUNKS = 4
BLOCK = 16


def dot(a, b, dims, precision=None):
    return lax.dot_general(a, b, (dims, ((), ())), precision=precision, preferred_element_type=F32)


def split(value):
    hi = value.astype(BF16)
    return hi, (value - hi.astype(F32)).astype(BF16)


class Net:
    def __init__(self, send_sem, recv_sem):
        self.send_sem, self.recv_sem = send_sem, recv_sem
        self.count = 0
        self.unsent = []

    def take(self, count):
        self.count += count
        return self.count - count

    def copy(self, slot, src, dst, device):
        return pltpu.make_async_remote_copy(
            src_ref=src,
            dst_ref=dst,
            send_sem=self.send_sem.at[slot],
            recv_sem=self.recv_sem.at[slot],
            device_id=device,
            device_id_type=pl.DeviceIdType.MESH,
        )

    def send(self, src, dst, device):
        copy = self.copy(self.take(1), src, dst, device)
        copy.start()
        self.unsent.append(copy)
        return copy

    def drain(self):
        for copy in self.unsent:
            copy.wait_send()
        self.unsent = []


def reciprocal(value):
    guess = pl.reciprocal(value, approx=True)
    guess = guess * (2.0 - value * guess)
    return guess * (2.0 - value * guess)


def inverse_factor(work, out):
    sub = lax.broadcasted_iota(jnp.int32, (BLOCK, K), 0)

    def step(b, carry):
        at = pl.multiple_of(b * BLOCK, BLOCK)
        gram = work[pl.ds(at, BLOCK), :K]
        inv = work[pl.ds(at, BLOCK), K:]
        turned = pltpu.roll(gram, lax.rem(K - at, K), 1)
        cols = [jnp.broadcast_to(turned[:, l : l + 1], (BLOCK, K)) for l in range(BLOCK)]
        pivots = jnp.ones((BLOCK, K), F32)
        for k in range(BLOCK):
            pivot = cols[k][k : k + 1, :]
            pivots = jnp.where(sub == k, pivot, pivots)
            mult = jnp.where(sub > k, cols[k] * reciprocal(pivot), 0.0)
            for l in range(k + 1, BLOCK):
                cols[l] = cols[l] - mult * cols[l][k : k + 1, :]
            gram = gram - mult * gram[k : k + 1, :]
            inv = inv - mult * inv[k : k + 1, :]
        scale = lax.rsqrt(pivots)
        scale = scale * (1.5 - 0.5 * pivots * scale * scale)
        gram = gram * scale
        inv = inv * scale
        out[pl.ds(at, BLOCK), :] = inv
        both = jnp.concatenate([gram, inv], axis=1)
        work[...] = work[...] - dot(gram, both, ((0,), (0,)), HIGH)
        return carry

    lax.fori_loop(0, K // BLOCK, step, 0)


def kernel(
    dims, emb, sketch, basis, panel_t,
    e_v, om_v, y_v, zt, zc, colsum, buf, part, core_in, land1, land2, zsrc, z_in,
    sr, sr_core, sr_x, y_src, sr_y, z_rec, sr_z, m3c, mzc, corr, gram, work, fac, ph,
    load_sem, send_sem, recv_sem,
):
    X, Y, Z = dims
    rows = emb.shape[0]
    width = emb.shape[1]
    chunk = rows // CHUNKS
    share = K // Z

    def load(i):
        piece = pl.ds(pl.multiple_of(i * chunk, chunk), chunk)
        return pltpu.make_async_copy(emb.at[piece], e_v.at[piece], load_sem.at[i])

    load_sketch = pltpu.make_async_copy(sketch, om_v, load_sem.at[CHUNKS])
    load_sketch.start()
    for i in range(CHUNKS):
        load(i).start()

    a, b = lax.axis_index("rowa"), lax.axis_index("rowb")
    x, c = a // 2, a % 2
    y, z = b // Z, b % Z

    def dev(dx=0, dc=0, dy=0, dz=0):
        return (((x + dx) % X) * 2 + (c + dc) % 2, ((y + dy) % Y) * Z + (z + dz) % Z)

    core_peer = dev(dc=1)
    x_peers = [dev(dx=k) for k in range(1, X)]
    y_peers = [dev(dy=k) for k in range(1, Y)]
    z_peers = [dev(dz=k) for k in range(1, Z)]
    peers = [core_peer] + x_peers + y_peers + z_peers
    barrier = pltpu.get_barrier_semaphore()
    for peer in peers:
        pl.semaphore_signal(barrier, inc=1, device_id=peer, device_id_type=pl.DeviceIdType.MESH)

    net = Net(send_sem, recv_sem)
    sub = lax.broadcasted_iota(jnp.int32, (8, K), 0)

    def group_mean(tile_rows, count):
        return jnp.sum(tile_rows, axis=0, keepdims=True) * (1.0 / count)

    def outer(left, right):
        return dot(left, right, ((0,), (0,)), HIGH)

    def sketch_chunk(i, carry):
        load(i).wait()
        piece = pl.ds(pl.multiple_of(i * chunk, chunk), chunk)
        y_v[piece, :] = dot(e_v[piece, :], om_v[...], ((1,), (0,)))
        block = e_v[piece, :].astype(F32)
        colsum[...] = colsum[...] + jnp.sum(block.reshape(chunk // 8, 8, width), axis=0)
        return carry

    colsum[...] = jnp.zeros_like(colsum)
    load_sketch.wait()
    lax.fori_loop(0, CHUNKS, sketch_chunk, 0)

    def center():
        first = jnp.sum(y_v[...], axis=0, keepdims=True) * (1.0 / rows)
        value = y_v[...] - first
        rest = jnp.sum(value, axis=0, keepdims=True) * (1.0 / rows)
        y_v[...] = value - rest
        return first + rest

    def products(core, xx, add):
        def step(half, carry):
            at = pl.multiple_of(((xx * 2 + core) * Y + 2 * half) * K, 2 * K)
            prod = dot(zt[...], e_v[:, pl.ds(at, 2 * K)], ((1,), (0,)))
            prod = prod[:K] + prod[K:]
            for k in range(2):
                yy = 2 * half + k
                top = prod[: K // 2, k * K : (k + 1) * K]
                low = prod[K // 2 :, k * K : (k + 1) * K]
                if add is None:
                    part[0, xx, yy] = top
                    part[1, yy, xx] = low
                else:
                    buf[0, xx, yy] = top + core_in[add, 0, xx, yy]
                    buf[1, yy, xx] = low + core_in[add, 1, yy, xx]
            return carry

        lax.fori_loop(0, Y // 2, step, 0)

    def reduce(p, local_mean):
        shift = center()
        hi, lo = split(y_v[...])
        zc[:, :K] = hi
        zc[:, K:] = lo
        zt[...] = zc[...].T
        four = dot(zt[...], zc[...], ((1,), (0,)))
        full = (four[:K, :K] + four[K:, K:]) + (four[:K, K:] + four[K:, :K])
        count = 24 if local_mean is None else 24 + 8 * Y
        for cc in range(2):
            for xx in range(X):
                sr[cc, xx, 0:16] = full[(cc * X + xx) * 16 : (cc * X + xx + 1) * 16]
                sr[cc, xx, 16:24] = jnp.where(sub == a, shift, 0.0)
                if local_mean is not None:
                    for yy in range(Y):
                        j = (xx * 2 + cc) * Y + yy
                        tile = jnp.where(sub == a, local_mean[:, j * K : (j + 1) * K], 0.0)
                        sr[cc, xx, 24 + 8 * yy : 32 + 8 * yy] = tile
        if p == 0:
            pl.semaphore_wait(barrier, len(peers))
        head, tail = pl.ds(0, 24), pl.ds(24, 8 * Y)
        flight = [net.send(sr.at[1 - c, :, head], sr_core.at[p, :, head], core_peer)]
        if local_mean is not None:
            flight.append(net.send(sr.at[1 - c, :, tail], sr_core.at[p, :, tail], core_peer))

        base = net.take(2 * X)

        def panels(j):
            xx = lax.rem(x + X - 1 - j, X)
            return [
                net.copy(base + 2 * j, part.at[0, xx], core_in.at[p, 0, xx], core_peer),
                net.copy(base + 2 * j + 1, part.at[1, :, xx], core_in.at[p, 1, :, xx], core_peer),
            ]

        def partner(j, carry):
            products(1 - c, lax.rem(x + X - 1 - j, X), None)
            for copy in panels(j):
                copy.start()
            return carry

        lax.fori_loop(0, 1, partner, 0)
        for copy in flight:
            copy.wait_recv()
        rows_in = pl.ds(0, count)
        sr[c, :, rows_in] = sr[c, :, rows_in] + sr_core[p, :, rows_in]
        xf = [
            net.send(sr.at[c, (x + k + 1) % X, head], sr_x.at[p, k, head], peer)
            for k, peer in enumerate(x_peers)
        ]
        if local_mean is not None:
            xf += [
                net.send(sr.at[c, (x + k + 1) % X, tail], sr_x.at[p, k, tail], peer)
                for k, peer in enumerate(x_peers)
            ]
        lax.fori_loop(1, X, partner, 0)

        base_a = net.take(X - 1)

        def first_a(j):
            k = X - 1 - j
            return net.copy(
                base_a + j, buf.at[0, lax.rem(x + k, X)], land1.at[p, 0, j], dev(dx=k)
            )

        def own(j, carry):
            for copy in panels(j):
                copy.wait_recv()
            products(c, lax.rem(x + X - 1 - j, X), p)

            @pl.when(j < X - 1)
            def _():
                first_a(j).start()

            return carry

        lax.fori_loop(0, X, own, 0)

        record = sr[c, x, rows_in]
        for copy in xf:
            copy.wait_recv()
        for k in range(X - 1):
            record = record + sr_x[p, k, rows_in]
        y_src[p, rows_in] = record
        yf = [
            net.send(y_src.at[p, head], sr_y.at[p, k, head], peer) for k, peer in enumerate(y_peers)
        ]
        if local_mean is not None:
            for k, peer in enumerate(y_peers):
                tile = pl.ds(pl.multiple_of(24 + 8 * ((y + k + 1) % Y), 8), 8)
                yf.append(net.send(y_src.at[p, tile], sr_y.at[p, k, pl.ds(24, 8)], peer))
        first_b = [
            net.send(buf.at[1, (y + k) % Y], land1.at[p, 1, k - 1], y_peers[k - 1]) for k in (2, 1, 3)
        ]
        for copy in yf:
            copy.wait_recv()
        own_gram = y_src[p, 0:16]
        shifts = [y_src[p, 16:24]]
        for k in range(Y - 1):
            own_gram = own_gram + sr_y[p, k, 0:16]
            shifts.append(sr_y[p, k, 16:24])
        shifts = jnp.concatenate(shifts, axis=0)
        group_shift = group_mean(shifts, 8 * Y)
        shifts = shifts - group_shift
        if local_mean is not None:
            means = [y_src[p, pl.ds(pl.multiple_of(24 + 8 * y, 8), 8)]]
            means += [sr_y[p, k, 24:32] for k in range(Y - 1)]
            means = jnp.concatenate(means, axis=0)
            group = group_mean(means, 8 * Y)
            m3c[...] = means - group
        else:
            group = group_shift
        place = pl.ds(pl.multiple_of((c * X + x) * 16, 16), 16)
        corr[0] = outer(shifts, shifts) * rows
        z_rec[p, 0:16] = own_gram + corr[0, place, :]
        z_rec[p, 16:24] = jnp.where(sub == 0, group, jnp.where(sub == 1, group_shift, 0.0))
        zf = [net.send(z_rec.at[p], sr_z.at[p, k], peer) for k, peer in enumerate(z_peers)]
        corr[1] = outer(m3c[...], shifts) * rows

        def collect(g, at, copies, land):
            ref = buf.at[g, at[0]] if len(at) == 1 else buf.at[g, at[0], at[1]]
            total = ref[...]
            for copy in copies:
                copy.wait_recv()
            for k in range(RING - 1):
                total = total + land[p, g, k]
            ref[...] = total

        collect(0, (x,), [first_a(j) for j in range(X - 1)], land1)
        second_a = [
            net.send(buf.at[0, x, (y + k) % Y], land2.at[p, 0, k - 1], y_peers[k - 1]) for k in (2, 1, 3)
        ]
        collect(1, (y,), first_b, land1)
        second_b = [
            net.send(buf.at[1, y, (x + k) % X], land2.at[p, 1, k - 1], x_peers[k - 1]) for k in (2, 1, 3)
        ]

        total = z_rec[p, 0:16]
        tiles = [z_rec[p, 16:24]]
        for k, copy in enumerate(zf):
            copy.wait_recv()
            total = total + sr_z[p, k, 0:16]
            tiles.append(sr_z[p, k, 16:24])
        gram[p, place, :] = total
        gf = [net.send(gram.at[p, place], gram.at[p, place], peer) for peer in x_peers]
        mz = jnp.zeros((8, K), F32)
        sz = jnp.zeros((8, K), F32)
        for k, tile in enumerate(tiles):
            mz = jnp.where(sub == k, tile[0:1], mz)
            sz = jnp.where(sub == k, tile[1:2], sz)
        mean_shift = group_mean(sz, Z)
        sz = jnp.where(sub < Z, sz - mean_shift, 0.0)
        if local_mean is not None:
            mzc[...] = jnp.where(sub < Z, mz - group_mean(mz, Z), 0.0)
        weight = float(rows * 2 * X * Y)
        corr[2] = outer(mzc[...], sz) * weight
        corr[0] = outer(sz, sz) * weight

        collect(0, (x, y), second_a, land2)
        collect(1, (y, x), second_b, land2)
        zsrc[:, : K // 2] = buf[0, x, y].T + corr[1, :, : K // 2]
        zsrc[:, K // 2 :] = buf[1, y, x].T + corr[1, :, K // 2 :]
        pf = [
            net.send(
                zsrc.at[pl.ds(pl.multiple_of(((z + k + 1) % Z) * share, share), share)],
                z_in.at[p, k],
                peer,
            )
            for k, peer in enumerate(z_peers)
        ]
        for copy in gf:
            copy.wait_recv()
        place = pl.ds(pl.multiple_of(c * (K // 2), K // 2), K // 2)
        last = net.send(gram.at[p, place], gram.at[p, place], core_peer)
        eye = lax.broadcasted_iota(jnp.int32, (K, K), 0) == lax.broadcasted_iota(jnp.int32, (K, K), 1)
        work[:, K:] = eye.astype(F32)
        last.wait_recv()
        work[:, :K] = gram[p] + corr[0]
        inverse_factor(work, fac)
        place = pl.ds(pl.multiple_of(z * share, share), share)
        mine = zsrc[place, :] + corr[2, place, :]
        for k, copy in enumerate(pf):
            copy.wait_recv()
            mine = mine + z_in[p, k]
        net.drain()
        for j in range(X):
            for copy in panels(j):
                copy.wait_send()
        for j in range(X - 1):
            first_a(j).wait_send()
        return mine, shift - mean_shift

    local_mean = jnp.sum(colsum[...], axis=0, keepdims=True) * (1.0 / rows)
    mine, _ = reduce(0, local_mean)
    panel = dot(mine, fac[...], ((1,), (1,)), HIGH).astype(BF16)
    place = pl.ds(pl.multiple_of(z * share, share), share)
    ph[x, c, y, place, :] = panel
    flight = [net.send(ph.at[x, c, y, place], ph.at[x, c, y, place], peer) for peer in z_peers]
    for copy in flight:
        copy.wait_recv()
    low, high = pl.ds(0, K // 2), pl.ds(K // 2, K // 2)
    near, far = ph.at[x, c, y, low], ph.at[x, c, y, high]
    flight_a = [net.send(near, near, y_peers[k - 1]) for k in (2, 1, 3)]
    flight_b = [net.send(far, far, x_peers[k - 1]) for k in (2, 1, 3)]
    for copy in flight_a:
        copy.wait_recv()
    near, far = ph.at[x, c, :, low], ph.at[:, c, y, high]
    flight_a = [net.send(near, near, x_peers[k - 1]) for k in (2, 1, 3)]
    for copy in flight_b:
        copy.wait_recv()
    flight_b = [net.send(far, far, y_peers[k - 1]) for k in (2, 1, 3)]
    for copy in flight_a:
        copy.wait_recv()
    near, far = ph.at[:, c, :, low], ph.at[:, c, :, high]
    last = [net.send(near, near, core_peer)]
    for copy in flight_b:
        copy.wait_recv()
    last.append(net.send(far, far, core_peer))

    def second(core):
        def step(xx, carry):
            at = pl.multiple_of((xx * 2 + core) * Y * K, Y * K)
            right = ph[xx, core].reshape(Y * K, K)
            y_v[...] = y_v[...] + dot(e_v[:, pl.ds(at, Y * K)], right, ((1,), (0,)))
            return carry

        lax.fori_loop(0, X, step, 0)

    y_v[...] = jnp.zeros_like(y_v)
    second(c)
    for copy in last:
        copy.wait_recv()
    second(1 - c)
    net.drain()

    mine, offset = reduce(1, None)
    root = jnp.sqrt(jnp.full((1, K), rows * 2 * X * Y * Z, F32))
    basis[...] = dot(y_v[...] + offset, fac[...], ((1,), (1,)), HIGH) * root
    panel_t[...] = dot(mine, fac[...], ((1,), (1,)), HIGH) / root


def hand_on(basis_in, panel_in, basis_out, panel_out):
    basis_out[...] = basis_in[...]
    panel_out[...] = panel_in[...]


def on_device(dims, embeddings, sketch):
    X, Y, Z = dims
    rows, width = embeddings.shape
    share = K // Z
    record = 24 + 8 * Y
    vm = pltpu.VMEM
    transfers = 2 * (18 + 6 * (X + Y) + 2 * Z) + Z + 2 * (X + Y)
    results = pl.pallas_call(
        functools.partial(kernel, dims),
        out_shape=(
            jax.ShapeDtypeStruct((rows, K), F32),
            jax.ShapeDtypeStruct((share, K), F32),
        ),
        in_specs=[pl.BlockSpec(memory_space=pl.ANY)] * 2,
        out_specs=(pl.BlockSpec(memory_space=vm), pl.BlockSpec(memory_space=vm)),
        scratch_shapes=[
            vm((rows, width), BF16),
            vm((width, K), BF16),
            vm((rows, K), F32),
            vm((2 * K, rows), BF16),
            vm((rows, 2 * K), BF16),
            vm((8, width), F32),
            vm((2, RING, RING, K // 2, K), F32),
            vm((2, RING, RING, K // 2, K), F32),
            vm((2, 2, RING, RING, K // 2, K), F32),
            vm((2, 2, RING - 1, RING, K // 2, K), F32),
            vm((2, 2, RING - 1, K // 2, K), F32),
            vm((K, K), F32),
            vm((2, Z - 1, share, K), F32),
            vm((2, X, record, K), F32),
            vm((2, X, record, K), F32),
            vm((2, X - 1, record, K), F32),
            vm((2, record, K), F32),
            vm((2, Y - 1, 32, K), F32),
            vm((2, 24, K), F32),
            vm((2, Z - 1, 24, K), F32),
            vm((8 * Y, K), F32),
            vm((8, K), F32),
            vm((3, K, K), F32),
            vm((2, K, K), F32),
            vm((K, 2 * K), F32),
            vm((K, K), F32),
            vm((X, 2, Y, K, K), BF16),
            pltpu.SemaphoreType.DMA((CHUNKS + 1,)),
            pltpu.SemaphoreType.DMA((transfers,)),
            pltpu.SemaphoreType.DMA((transfers,)),
        ],
        compiler_params=pltpu.CompilerParams(
            collective_id=0, has_side_effects=True, vmem_limit_bytes=56 * 1024 * 1024
        ),
        name="pca",
    )(embeddings, sketch)
    return pl.pallas_call(
        hand_on,
        out_shape=[jax.ShapeDtypeStruct(value.shape, F32) for value in results],
        in_specs=[pl.BlockSpec(memory_space=vm)] * 2,
        out_specs=[pl.BlockSpec(memory_space=vm)] * 2,
        name="hand_on",
    )(*results)


def solution(mesh):
    X, Y = mesh.shape["rowa"] // 2, 4
    dims = (X, Y, mesh.shape["rowb"] // Y)
    spread = P(("rowa", "rowb"), None)
    return jax.shard_map(
        functools.partial(on_device, dims),
        mesh=mesh,
        in_specs=(spread, P()),
        out_specs=(spread, spread),
        check_vma=False,
    )
```

```python
import functools

import jax
import jax.numpy as jnp
from jax import lax
from jax.experimental import pallas as pl
from jax.experimental.pallas import tpu as pltpu
from jax.sharding import PartitionSpec as P

F32 = jnp.float32
BF16 = jnp.bfloat16
HIGH = lax.Precision.HIGHEST
K = 128
RING = 4
CHUNKS = 4
BLOCK = 32


def dot(a, b, dims, precision=None):
    return lax.dot_general(a, b, (dims, ((), ())), precision=precision, preferred_element_type=F32)


def split(value):
    hi = value.astype(BF16)
    return hi, (value - hi.astype(F32)).astype(BF16)


class Net:
    def __init__(self, send_sem, recv_sem):
        self.send_sem, self.recv_sem = send_sem, recv_sem
        self.count = 0
        self.unsent = []

    def take(self, count):
        self.count += count
        return self.count - count

    def copy(self, slot, src, dst, device):
        return pltpu.make_async_remote_copy(
            src_ref=src,
            dst_ref=dst,
            send_sem=self.send_sem.at[slot],
            recv_sem=self.recv_sem.at[slot],
            device_id=device,
            device_id_type=pl.DeviceIdType.MESH,
        )

    def send(self, src, dst, device):
        copy = self.copy(self.take(1), src, dst, device)
        copy.start()
        self.unsent.append(copy)
        return copy

    def drain(self):
        for copy in self.unsent:
            copy.wait_send()
        self.unsent = []


def reciprocal(value):
    guess = pl.reciprocal(value, approx=True)
    return guess * (2.0 - value * guess)


def inverse_factor(work, out):
    sub = lax.broadcasted_iota(jnp.int32, (BLOCK, K), 0)
    count = K // BLOCK
    both = [work[i * BLOCK : (i + 1) * BLOCK, :] for i in range(count)]
    for b in range(count):
        gram, inv = both[b][:, :K], both[b][:, K:]
        at = b * BLOCK
        cols = [jnp.broadcast_to(gram[:, at + l : at + l + 1], (BLOCK, K)) for l in range(BLOCK)]
        pivots = jnp.ones((BLOCK, K), F32)
        for k in range(BLOCK):
            pivot = cols[k][k : k + 1, :]
            pivots = jnp.where(sub == k, pivot, pivots)
            mult = jnp.where(sub > k, cols[k] * reciprocal(pivot), 0.0)
            for l in range(k + 1, BLOCK):
                cols[l] = cols[l] - mult * cols[l][k : k + 1, :]
            gram = gram - mult * gram[k : k + 1, :]
            inv = inv - mult * inv[k : k + 1, :]
        scale = lax.rsqrt(pivots)
        scale = scale * (1.5 - 0.5 * pivots * scale * scale)
        gram = gram * scale
        inv = inv * scale
        out[at : at + BLOCK, :] = inv
        full = jnp.concatenate([gram, inv], axis=1)
        for start, stop in ((b + 1, b + 2), (b + 2, count)):
            if start < min(stop, count):
                left = gram[:, start * BLOCK : stop * BLOCK]
                update = dot(left, full, ((0,), (0,)), HIGH)
                for i in range(start, stop):
                    both[i] = both[i] - update[(i - start) * BLOCK : (i - start + 1) * BLOCK]


def kernel(
    dims, emb, sketch, basis, panel_t,
    e_v, om_v, y_v, zt, zc, buf, part, core_in, land1, land2, zsrc, z_in,
    sr, sr_core, sr_x, y_src, sr_y, z_rec, sr_z, m3c, mzc, m_src, m_in, corr, gram, work, fac, ph,
    load_sem, send_sem, recv_sem,
):
    X, Y, Z = dims
    rows = emb.shape[0]
    width = emb.shape[1]
    chunk = rows // CHUNKS
    share = K // Z

    def load(i):
        piece = pl.ds(pl.multiple_of(i * chunk, chunk), chunk)
        return pltpu.make_async_copy(emb.at[piece], e_v.at[piece], load_sem.at[i])

    load_sketch = pltpu.make_async_copy(sketch, om_v, load_sem.at[CHUNKS])
    load_sketch.start()
    for i in range(CHUNKS):
        load(i).start()

    a, b = lax.axis_index("rowa"), lax.axis_index("rowb")
    x, c = a // 2, a % 2
    y, z = b // Z, b % Z

    def dev(dx=0, dc=0, dy=0, dz=0):
        return (((x + dx) % X) * 2 + (c + dc) % 2, ((y + dy) % Y) * Z + (z + dz) % Z)

    core_peer = dev(dc=1)
    x_peers = [dev(dx=k) for k in range(1, X)]
    y_peers = [dev(dy=k) for k in range(1, Y)]
    z_peers = [dev(dz=k) for k in range(1, Z)]
    peers = [core_peer] + x_peers + y_peers + z_peers
    barrier = pltpu.get_barrier_semaphore()
    for peer in peers:
        pl.semaphore_signal(barrier, inc=1, device_id=peer, device_id_type=pl.DeviceIdType.MESH)

    net = Net(send_sem, recv_sem)
    sub = lax.broadcasted_iota(jnp.int32, (8, K), 0)

    def group_mean(tile_rows, count):
        return jnp.sum(tile_rows, axis=0, keepdims=True) * (1.0 / count)

    def outer(left, right):
        return dot(left, right, ((0,), (0,)), HIGH)

    def sketch_chunk(i, carry):
        load(i).wait()
        piece = pl.ds(pl.multiple_of(i * chunk, chunk), chunk)
        y_v[piece, :] = dot(e_v[piece, :], om_v[...], ((1,), (0,)))
        return carry

    zt[2 * K :] = jnp.ones((16, rows), BF16)
    load_sketch.wait()
    lax.fori_loop(0, CHUNKS, sketch_chunk, 0)

    def center():
        first = jnp.sum(y_v[...], axis=0, keepdims=True) * (1.0 / rows)
        value = y_v[...] - first
        rest = jnp.sum(value, axis=0, keepdims=True) * (1.0 / rows)
        y_v[...] = value - rest
        return first + rest

    def products(core, xx, add, first):
        def step(half, carry):
            at = pl.multiple_of(((xx * 2 + core) * Y + 2 * half) * K, 2 * K)
            left = zt[...] if first else zt[: 2 * K]
            prod = dot(left, e_v[:, pl.ds(at, 2 * K)], ((1,), (0,)))
            sums = prod[2 * K : 2 * K + 1] * (1.0 / rows) if first else None
            prod = prod[:K] + prod[K : 2 * K]
            for k in range(2):
                yy = 2 * half + k
                if first:
                    tile = pl.ds(pl.multiple_of(24 + 8 * yy, 8), 8)
                    sr[core, xx, tile] = jnp.where(sub == a, sums[:, k * K : (k + 1) * K], 0.0)
                top = prod[: K // 2, k * K : (k + 1) * K]
                low = prod[K // 2 :, k * K : (k + 1) * K]
                if add is None:
                    part[0, xx, yy] = top
                    part[1, yy, xx] = low
                else:
                    buf[0, xx, yy] = top + core_in[add, 0, xx, yy]
                    buf[1, yy, xx] = low + core_in[add, 1, yy, xx]
            return carry

        lax.fori_loop(0, Y // 2, step, 0)

    def reduce(p):
        first = p == 0
        shift = center()
        hi, lo = split(y_v[...])
        zc[:, :K] = hi
        zc[:, K:] = lo
        zt[: 2 * K] = zc[...].T
        four = dot(zt[: 2 * K], zc[...], ((1,), (0,)))
        full = (four[:K, :K] + four[K:, K:]) + (four[:K, K:] + four[K:, :K])
        for cc in range(2):
            for xx in range(X):
                sr[cc, xx, 0:16] = full[(cc * X + xx) * 16 : (cc * X + xx + 1) * 16]
                sr[cc, xx, 16:24] = jnp.where(sub == a, shift, 0.0)
        if first:
            pl.semaphore_wait(barrier, len(peers))
        head, tail = pl.ds(0, 24), pl.ds(24, 8 * Y)
        flight = net.send(sr.at[1 - c, :, head], sr_core.at[p, :, head], core_peer)

        base = net.take(2 * X)

        def panels(j):
            xx = lax.rem(x + X - 1 - j, X)
            return [
                net.copy(base + 2 * j, part.at[0, xx], core_in.at[p, 0, xx], core_peer),
                net.copy(base + 2 * j + 1, part.at[1, :, xx], core_in.at[p, 1, :, xx], core_peer),
            ]

        def partner(j, carry):
            products(1 - c, lax.rem(x + X - 1 - j, X), None, first)
            for copy in panels(j):
                copy.start()
            return carry

        lax.fori_loop(0, 1, partner, 0)
        flight.wait_recv()
        sr[c, :, head] = sr[c, :, head] + sr_core[p, :, head]
        xf = [
            net.send(sr.at[c, (x + k + 1) % X, head], sr_x.at[p, k, head], peer)
            for k, peer in enumerate(x_peers)
        ]
        lax.fori_loop(1, X, partner, 0)
        if first:
            flight = net.send(sr.at[1 - c, :, tail], sr_core.at[p, :, tail], core_peer)

        base_a = net.take(X - 1)

        def first_a(j):
            k = X - 1 - j
            return net.copy(
                base_a + j, buf.at[0, lax.rem(x + k, X)], land1.at[p, 0, j], dev(dx=k)
            )

        def own(j, carry):
            for copy in panels(j):
                copy.wait_recv()
            products(c, lax.rem(x + X - 1 - j, X), p, first)

            @pl.when(j < X - 1)
            def _():
                first_a(j).start()

            return carry

        lax.fori_loop(0, X, own, 0)

        record = sr[c, x, head]
        for copy in xf:
            copy.wait_recv()
        for k in range(X - 1):
            record = record + sr_x[p, k, head]
        y_src[p, head] = record
        yf = [
            net.send(y_src.at[p, head], sr_y.at[p, k, head], peer) for k, peer in enumerate(y_peers)
        ]
        first_b = [
            net.send(buf.at[1, (y + k) % Y], land1.at[p, 1, k - 1], y_peers[k - 1]) for k in (2, 1, 3)
        ]
        if first:
            flight.wait_recv()
            sr[c, :, tail] = sr[c, :, tail] + sr_core[p, :, tail]
            xt = [
                net.send(sr.at[c, (x + k + 1) % X, tail], sr_x.at[p, k, tail], peer)
                for k, peer in enumerate(x_peers)
            ]
        for copy in yf:
            copy.wait_recv()
        own_gram = y_src[p, 0:16]
        shifts = [y_src[p, 16:24]]
        for k in range(Y - 1):
            own_gram = own_gram + sr_y[p, k, 0:16]
            shifts.append(sr_y[p, k, 16:24])
        shifts = jnp.concatenate(shifts, axis=0)
        group_shift = group_mean(shifts, 8 * Y)
        shifts = shifts - group_shift
        place = pl.ds(pl.multiple_of((c * X + x) * 16, 16), 16)
        corr[0] = outer(shifts, shifts) * rows
        z_rec[p, 0:16] = own_gram + corr[0, place, :]
        z_rec[p, 16:24] = jnp.broadcast_to(group_shift, (8, K))
        zf = [net.send(z_rec.at[p], sr_z.at[p, k], peer) for k, peer in enumerate(z_peers)]

        def collect(g, at, copies, land):
            ref = buf.at[g, at[0]] if len(at) == 1 else buf.at[g, at[0], at[1]]
            total = ref[...]
            for copy in copies:
                copy.wait_recv()
            for k in range(RING - 1):
                total = total + land[p, g, k]
            ref[...] = total

        collect(0, (x,), [first_a(j) for j in range(X - 1)], land1)
        second_a = [
            net.send(buf.at[0, x, (y + k) % Y], land2.at[p, 0, k - 1], y_peers[k - 1]) for k in (2, 1, 3)
        ]
        if first:
            for copy in xt:
                copy.wait_recv()
            means = sr[c, x, tail]
            for k in range(X - 1):
                means = means + sr_x[p, k, tail]
            y_src[p, tail] = means
            yt = []
            for k, peer in enumerate(y_peers):
                tile = pl.ds(pl.multiple_of(24 + 8 * ((y + k + 1) % Y), 8), 8)
                yt.append(net.send(y_src.at[p, tile], sr_y.at[p, k, pl.ds(24, 8)], peer))
        collect(1, (y,), first_b, land1)
        second_b = [
            net.send(buf.at[1, y, (x + k) % X], land2.at[p, 1, k - 1], x_peers[k - 1]) for k in (2, 1, 3)
        ]

        total = z_rec[p, 0:16]
        tiles = [z_rec[p, 16:24]]
        for k, copy in enumerate(zf):
            copy.wait_recv()
            total = total + sr_z[p, k, 0:16]
            tiles.append(sr_z[p, k, 16:24])
        gram[p, place, :] = total
        gf = [net.send(gram.at[p, place], gram.at[p, place], peer) for peer in x_peers]

        def by_group(tiles):
            value = jnp.zeros((8, K), F32)
            for k, tile in enumerate(tiles):
                value = jnp.where(sub == k, tile, value)
            mean = group_mean(value, Z)
            return jnp.where(sub < Z, value - mean, 0.0), mean

        sz, mean_shift = by_group(tiles)
        weight = float(rows * 2 * X * Y)
        corr[0] = outer(sz, sz) * weight
        if first:
            for copy in yt:
                copy.wait_recv()
            means = [y_src[p, pl.ds(pl.multiple_of(24 + 8 * y, 8), 8)]]
            means += [sr_y[p, k, 24:32] for k in range(Y - 1)]
            means = jnp.concatenate(means, axis=0)
            group = group_mean(means, 8 * Y)
            m3c[...] = means - group
            m_src[...] = jnp.broadcast_to(group, (8, K))
            zt_flight = [net.send(m_src, m_in.at[k], peer) for k, peer in enumerate(z_peers)]
        else:
            corr[2] = outer(mzc[...], sz) * weight
        corr[1] = outer(m3c[...], shifts) * rows
        for copy in gf:
            copy.wait_recv()
        place = pl.ds(pl.multiple_of(c * (K // 2), K // 2), K // 2)
        last = net.send(gram.at[p, place], gram.at[p, place], core_peer)

        collect(0, (x, y), second_a, land2)
        collect(1, (y, x), second_b, land2)
        zsrc[:, : K // 2] = buf[0, x, y].T + corr[1, :, : K // 2]
        zsrc[:, K // 2 :] = buf[1, y, x].T + corr[1, :, K // 2 :]
        pf = [
            net.send(
                zsrc.at[pl.ds(pl.multiple_of(((z + k + 1) % Z) * share, share), share)],
                z_in.at[p, k],
                peer,
            )
            for k, peer in enumerate(z_peers)
        ]
        eye = lax.broadcasted_iota(jnp.int32, (K, K), 0) == lax.broadcasted_iota(jnp.int32, (K, K), 1)
        work[:, K:] = eye.astype(F32)
        last.wait_recv()
        work[:, :K] = gram[p] + corr[0]
        inverse_factor(work, fac)
        if first:
            for copy in zt_flight:
                copy.wait_recv()
            mzc[...], _ = by_group([m_src[...]] + [m_in[k] for k in range(Z - 1)])
            corr[2] = outer(mzc[...], sz) * weight
        place = pl.ds(pl.multiple_of(z * share, share), share)
        mine = zsrc[place, :] + corr[2, place, :]
        for k, copy in enumerate(pf):
            copy.wait_recv()
            mine = mine + z_in[p, k]
        net.drain()
        for j in range(X):
            for copy in panels(j):
                copy.wait_send()
        for j in range(X - 1):
            first_a(j).wait_send()
        return mine, shift - mean_shift

    mine, _ = reduce(0)
    panel = dot(mine, fac[...], ((1,), (1,)), HIGH).astype(BF16)
    place = pl.ds(pl.multiple_of(z * share, share), share)
    ph[x, c, y, place, :] = panel
    flight = [net.send(ph.at[x, c, y, place], ph.at[x, c, y, place], peer) for peer in z_peers]
    for copy in flight:
        copy.wait_recv()
    low, high = pl.ds(0, K // 2), pl.ds(K // 2, K // 2)
    near, far = ph.at[x, c, y, low], ph.at[x, c, y, high]
    flight_a = [net.send(near, near, y_peers[k - 1]) for k in (2, 1, 3)]
    flight_b = [net.send(far, far, x_peers[k - 1]) for k in (2, 1, 3)]
    for copy in flight_a:
        copy.wait_recv()
    near, far = ph.at[x, c, :, low], ph.at[:, c, y, high]
    flight_a = [net.send(near, near, x_peers[k - 1]) for k in (2, 1, 3)]
    for copy in flight_b:
        copy.wait_recv()
    flight_b = [net.send(far, far, y_peers[k - 1]) for k in (2, 1, 3)]
    for copy in flight_a:
        copy.wait_recv()
    near, far = ph.at[:, c, :, low], ph.at[:, c, :, high]
    last = [net.send(near, near, core_peer)]
    for copy in flight_b:
        copy.wait_recv()
    last.append(net.send(far, far, core_peer))

    def second(core):
        def step(xx, carry):
            at = pl.multiple_of((xx * 2 + core) * Y * K, Y * K)
            right = ph[xx, core].reshape(Y * K, K)
            y_v[...] = y_v[...] + dot(e_v[:, pl.ds(at, Y * K)], right, ((1,), (0,)))
            return carry

        lax.fori_loop(0, X, step, 0)

    y_v[...] = jnp.zeros_like(y_v)
    second(c)
    for copy in last:
        copy.wait_recv()
    second(1 - c)
    net.drain()

    mine, offset = reduce(1)
    root = jnp.sqrt(jnp.full((1, K), rows * 2 * X * Y * Z, F32))
    basis[...] = dot(y_v[...] + offset, fac[...], ((1,), (1,)), HIGH) * root
    panel_t[...] = dot(mine, fac[...], ((1,), (1,)), HIGH) / root


def hand_on(basis_in, panel_in, basis_out, panel_out):
    basis_out[...] = basis_in[...]
    panel_out[...] = panel_in[...]


def on_device(dims, embeddings, sketch):
    X, Y, Z = dims
    rows, width = embeddings.shape
    share = K // Z
    record = 24 + 8 * Y
    vm = pltpu.VMEM
    transfers = 2 * (18 + 6 * (X + Y) + 3 * Z) + Z + 2 * (X + Y)
    results = pl.pallas_call(
        functools.partial(kernel, dims),
        out_shape=(
            jax.ShapeDtypeStruct((rows, K), F32),
            jax.ShapeDtypeStruct((share, K), F32),
        ),
        in_specs=[pl.BlockSpec(memory_space=pl.ANY)] * 2,
        out_specs=(pl.BlockSpec(memory_space=vm), pl.BlockSpec(memory_space=vm)),
        scratch_shapes=[
            vm((rows, width), BF16),
            vm((width, K), BF16),
            vm((rows, K), F32),
            vm((2 * K + 16, rows), BF16),
            vm((rows, 2 * K), BF16),
            vm((2, RING, RING, K // 2, K), F32),
            vm((2, RING, RING, K // 2, K), F32),
            vm((2, 2, RING, RING, K // 2, K), F32),
            vm((2, 2, RING - 1, RING, K // 2, K), F32),
            vm((2, 2, RING - 1, K // 2, K), F32),
            vm((K, K), F32),
            vm((2, Z - 1, share, K), F32),
            vm((2, X, record, K), F32),
            vm((2, X, record, K), F32),
            vm((2, X - 1, record, K), F32),
            vm((2, record, K), F32),
            vm((2, Y - 1, 32, K), F32),
            vm((2, 24, K), F32),
            vm((2, Z - 1, 24, K), F32),
            vm((8 * Y, K), F32),
            vm((8, K), F32),
            vm((8, K), F32),
            vm((Z - 1, 8, K), F32),
            vm((3, K, K), F32),
            vm((2, K, K), F32),
            vm((K, 2 * K), F32),
            vm((K, K), F32),
            vm((X, 2, Y, K, K), BF16),
            pltpu.SemaphoreType.DMA((CHUNKS + 1,)),
            pltpu.SemaphoreType.DMA((transfers,)),
            pltpu.SemaphoreType.DMA((transfers,)),
        ],
        compiler_params=pltpu.CompilerParams(
            collective_id=0, has_side_effects=True, vmem_limit_bytes=56 * 1024 * 1024
        ),
        name="pca",
    )(embeddings, sketch)
    return pl.pallas_call(
        hand_on,
        out_shape=[jax.ShapeDtypeStruct(value.shape, F32) for value in results],
        in_specs=[pl.BlockSpec(memory_space=vm)] * 2,
        out_specs=[pl.BlockSpec(memory_space=vm)] * 2,
        name="hand_on",
    )(*results)


def solution(mesh):
    X, Y = mesh.shape["rowa"] // 2, 4
    dims = (X, Y, mesh.shape["rowb"] // Y)
    spread = P(("rowa", "rowb"), None)
    return jax.shard_map(
        functools.partial(on_device, dims),
        mesh=mesh,
        in_specs=(spread, P()),
        out_specs=(spread, spread),
        check_vma=False,
    )
```

```python
import functools

import jax
import jax.numpy as jnp
from jax import lax
from jax.experimental import pallas as pl
from jax.experimental.pallas import tpu as pltpu
from jax.sharding import PartitionSpec as P

F32 = jnp.float32
BF16 = jnp.bfloat16
HIGH = lax.Precision.HIGHEST
K = 128
RING = 4
CHUNKS = 4
BLOCK = 32


def dot(a, b, dims, precision=None):
    return lax.dot_general(a, b, (dims, ((), ())), precision=precision, preferred_element_type=F32)


def split(value):
    hi = value.astype(BF16)
    return hi, (value - hi.astype(F32)).astype(BF16)


class Net:
    def __init__(self, send_sem, recv_sem):
        self.send_sem, self.recv_sem = send_sem, recv_sem
        self.count = 0
        self.unsent = []

    def take(self, count):
        self.count += count
        return self.count - count

    def copy(self, slot, src, dst, device):
        return pltpu.make_async_remote_copy(
            src_ref=src,
            dst_ref=dst,
            send_sem=self.send_sem.at[slot],
            recv_sem=self.recv_sem.at[slot],
            device_id=device,
            device_id_type=pl.DeviceIdType.MESH,
        )

    def send(self, src, dst, device):
        copy = self.copy(self.take(1), src, dst, device)
        copy.start()
        self.unsent.append(copy)
        return copy

    def drain(self):
        for copy in self.unsent:
            copy.wait_send()
        self.unsent = []


def reciprocal(value):
    guess = pl.reciprocal(value, approx=True)
    return guess * (2.0 - value * guess)


def inverse_factor(work, out):
    sub = lax.broadcasted_iota(jnp.int32, (BLOCK, K), 0)
    count = K // BLOCK
    both = [work[i * BLOCK : (i + 1) * BLOCK, :] for i in range(count)]
    for b in range(count):
        gram, inv = both[b][:, :K], both[b][:, K:]
        at = b * BLOCK
        cols = [jnp.broadcast_to(gram[:, at + l : at + l + 1], (BLOCK, K)) for l in range(BLOCK)]
        pivots = jnp.ones((BLOCK, K), F32)
        for k in range(BLOCK):
            pivot = cols[k][k : k + 1, :]
            pivots = jnp.where(sub == k, pivot, pivots)
            mult = jnp.where(sub > k, cols[k] * reciprocal(pivot), 0.0)
            for l in range(k + 1, BLOCK):
                cols[l] = cols[l] - mult * cols[l][k : k + 1, :]
            gram = gram - mult * gram[k : k + 1, :]
            inv = inv - mult * inv[k : k + 1, :]
        scale = lax.rsqrt(pivots)
        scale = scale * (1.5 - 0.5 * pivots * scale * scale)
        gram = gram * scale
        inv = inv * scale
        out[at : at + BLOCK, :] = inv
        full = jnp.concatenate([gram, inv], axis=1)
        for start, stop in ((b + 1, b + 2), (b + 2, count)):
            if start < min(stop, count):
                left = gram[:, start * BLOCK : stop * BLOCK]
                update = dot(left, full, ((0,), (0,)), HIGH)
                for i in range(start, stop):
                    both[i] = both[i] - update[(i - start) * BLOCK : (i - start + 1) * BLOCK]


def kernel(
    dims, emb, sketch, basis, panel_t,
    e_v, om_v, y_v, zt, zc, buf, part, core_in, land1, land2, zsrc, z_in,
    sr, sr_core, sr_x, y_src, sr_y, z_rec, sr_z, m3c, mzc, m_src, m_in, corr, gram, work, fac, ph,
    load_sem, send_sem, recv_sem,
):
    X, Y, Z = dims
    rows = emb.shape[0]
    width = emb.shape[1]
    chunk = rows // CHUNKS
    share = K // Z

    def load(i):
        piece = pl.ds(pl.multiple_of(i * chunk, chunk), chunk)
        return pltpu.make_async_copy(emb.at[piece], e_v.at[piece], load_sem.at[i])

    load_sketch = pltpu.make_async_copy(sketch, om_v, load_sem.at[CHUNKS])
    load_sketch.start()
    for i in range(CHUNKS):
        load(i).start()

    a, b = lax.axis_index("rowa"), lax.axis_index("rowb")
    x, c = a // 2, a % 2
    y, z = b // Z, b % Z

    def dev(dx=0, dc=0, dy=0, dz=0):
        return (((x + dx) % X) * 2 + (c + dc) % 2, ((y + dy) % Y) * Z + (z + dz) % Z)

    core_peer = dev(dc=1)
    x_peers = [dev(dx=k) for k in range(1, X)]
    y_peers = [dev(dy=k) for k in range(1, Y)]
    z_peers = [dev(dz=k) for k in range(1, Z)]
    peers = [core_peer] + x_peers + y_peers + z_peers
    barrier = pltpu.get_barrier_semaphore()
    for peer in peers:
        pl.semaphore_signal(barrier, inc=1, device_id=peer, device_id_type=pl.DeviceIdType.MESH)

    net = Net(send_sem, recv_sem)
    sub = lax.broadcasted_iota(jnp.int32, (8, K), 0)

    def group_mean(tile_rows, count):
        return jnp.sum(tile_rows, axis=0, keepdims=True) * (1.0 / count)

    def outer(left, right):
        return dot(left, right, ((0,), (0,)), HIGH)

    def sketch_chunk(i, carry):
        load(i).wait()
        piece = pl.ds(pl.multiple_of(i * chunk, chunk), chunk)
        y_v[piece, :] = dot(e_v[piece, :], om_v[...], ((1,), (0,)))
        return carry

    zt[2 * K :] = jnp.ones((16, rows), BF16)
    load_sketch.wait()
    lax.fori_loop(0, CHUNKS, sketch_chunk, 0)

    def center():
        first = jnp.sum(y_v[...], axis=0, keepdims=True) * (1.0 / rows)
        value = y_v[...] - first
        rest = jnp.sum(value, axis=0, keepdims=True) * (1.0 / rows)
        y_v[...] = value - rest
        return first + rest

    def products(core, xx, add, first):
        def step(half, carry):
            at = pl.multiple_of(((xx * 2 + core) * Y + 2 * half) * K, 2 * K)
            left = zt[...] if first else zt[: 2 * K]
            prod = dot(left, e_v[:, pl.ds(at, 2 * K)], ((1,), (0,)))
            sums = prod[2 * K : 2 * K + 1] * (1.0 / rows) if first else None
            prod = prod[:K] + prod[K : 2 * K]
            for k in range(2):
                yy = 2 * half + k
                if first:
                    tile = pl.ds(pl.multiple_of(24 + 8 * yy, 8), 8)
                    sr[core, xx, tile] = jnp.where(sub == a, sums[:, k * K : (k + 1) * K], 0.0)
                top = prod[: K // 2, k * K : (k + 1) * K]
                low = prod[K // 2 :, k * K : (k + 1) * K]
                if add is None:
                    part[0, xx, yy] = top
                    part[1, yy, xx] = low
                else:
                    buf[0, xx, yy] = top + core_in[add, 0, xx, yy]
                    buf[1, yy, xx] = low + core_in[add, 1, yy, xx]
            return carry

        lax.fori_loop(0, Y // 2, step, 0)

    def reduce(p):
        first = p == 0
        shift = center()
        hi, lo = split(y_v[...])
        zc[:, :K] = hi
        zc[:, K:] = lo
        zt[: 2 * K] = zc[...].T
        four = dot(zt[: 2 * K], zc[...], ((1,), (0,)))
        full = (four[:K, :K] + four[K:, K:]) + (four[:K, K:] + four[K:, :K])
        for cc in range(2):
            for xx in range(X):
                sr[cc, xx, 0:16] = full[(cc * X + xx) * 16 : (cc * X + xx + 1) * 16]
                sr[cc, xx, 16:24] = jnp.where(sub == a, shift, 0.0)
        if first:
            pl.semaphore_wait(barrier, len(peers))
        head, tail = pl.ds(0, 24), pl.ds(24, 8 * Y)
        flight = net.send(sr.at[1 - c, :, head], sr_core.at[p, :, head], core_peer)

        base = net.take(2 * X)

        def panels(j):
            xx = lax.rem(x + X - 1 - j, X)
            return [
                net.copy(base + 2 * j, part.at[0, xx], core_in.at[p, 0, xx], core_peer),
                net.copy(base + 2 * j + 1, part.at[1, :, xx], core_in.at[p, 1, :, xx], core_peer),
            ]

        def partner(j, carry):
            products(1 - c, lax.rem(x + X - 1 - j, X), None, first)
            for copy in panels(j):
                copy.start()
            return carry

        lax.fori_loop(0, 1, partner, 0)
        flight.wait_recv()
        sr[c, :, head] = sr[c, :, head] + sr_core[p, :, head]
        xf = [
            net.send(sr.at[c, (x + k + 1) % X, head], sr_x.at[p, k, head], peer)
            for k, peer in enumerate(x_peers)
        ]
        base_a = net.take(X - 1)
        base_b = net.take((Y - 1) * X)

        def first_a(j):
            k = X - 1 - j
            return net.copy(
                base_a + j, buf.at[0, lax.rem(x + k, X)], land1.at[p, 0, j], dev(dx=k)
            )

        def first_b(j, k):
            xx = lax.rem(x + X - 1 - j, X)
            return net.copy(
                base_b + (Y - 1) * j + k - 1,
                buf.at[1, lax.rem(y + k, Y), xx],
                land1.at[p, 1, k - 1, xx],
                y_peers[k - 1],
            )

        def own(j):
            for copy in panels(j):
                copy.wait_recv()
            products(c, lax.rem(x + X - 1 - j, X), p, first)
            for k in (2, 1, 3):
                first_b(j, k).start()

        def both(j, carry):
            partner(j, carry)
            own(j - 1)
            first_a(j - 1).start()
            return carry

        lax.fori_loop(1, X, both, 0)
        if first:
            flight = net.send(sr.at[1 - c, :, tail], sr_core.at[p, :, tail], core_peer)
        own(X - 1)

        record = sr[c, x, head]
        for copy in xf:
            copy.wait_recv()
        for k in range(X - 1):
            record = record + sr_x[p, k, head]
        y_src[p, head] = record
        yf = [
            net.send(y_src.at[p, head], sr_y.at[p, k, head], peer) for k, peer in enumerate(y_peers)
        ]
        if first:
            flight.wait_recv()
            sr[c, :, tail] = sr[c, :, tail] + sr_core[p, :, tail]
            xt = [
                net.send(sr.at[c, (x + k + 1) % X, tail], sr_x.at[p, k, tail], peer)
                for k, peer in enumerate(x_peers)
            ]
        for copy in yf:
            copy.wait_recv()
        own_gram = y_src[p, 0:16]
        shifts = [y_src[p, 16:24]]
        for k in range(Y - 1):
            own_gram = own_gram + sr_y[p, k, 0:16]
            shifts.append(sr_y[p, k, 16:24])
        shifts = jnp.concatenate(shifts, axis=0)
        group_shift = group_mean(shifts, 8 * Y)
        shifts = shifts - group_shift
        place = pl.ds(pl.multiple_of((c * X + x) * 16, 16), 16)
        corr[0] = outer(shifts, shifts) * rows
        z_rec[p, 0:16] = own_gram + corr[0, place, :]
        z_rec[p, 16:24] = jnp.broadcast_to(group_shift, (8, K))
        zf = [net.send(z_rec.at[p], sr_z.at[p, k], peer) for k, peer in enumerate(z_peers)]

        def collect(g, at, copies, land):
            ref = buf.at[g, at[0]] if len(at) == 1 else buf.at[g, at[0], at[1]]
            total = ref[...]
            for copy in copies:
                copy.wait_recv()
            for k in range(RING - 1):
                total = total + land[p, g, k]
            ref[...] = total

        collect(0, (x,), [first_a(j) for j in range(X - 1)], land1)
        second_a = [
            net.send(buf.at[0, x, (y + k) % Y], land2.at[p, 0, k - 1], y_peers[k - 1]) for k in (2, 1, 3)
        ]
        if first:
            for copy in xt:
                copy.wait_recv()
            means = sr[c, x, tail]
            for k in range(X - 1):
                means = means + sr_x[p, k, tail]
            y_src[p, tail] = means
            yt = []
            for k, peer in enumerate(y_peers):
                tile = pl.ds(pl.multiple_of(24 + 8 * ((y + k + 1) % Y), 8), 8)
                yt.append(net.send(y_src.at[p, tile], sr_y.at[p, k, pl.ds(24, 8)], peer))
        collect(1, (y,), [first_b(j, k) for j in range(X) for k in range(1, Y)], land1)
        second_b = [
            net.send(buf.at[1, y, (x + k) % X], land2.at[p, 1, k - 1], x_peers[k - 1]) for k in (2, 1, 3)
        ]

        total = z_rec[p, 0:16]
        tiles = [z_rec[p, 16:24]]
        for k, copy in enumerate(zf):
            copy.wait_recv()
            total = total + sr_z[p, k, 0:16]
            tiles.append(sr_z[p, k, 16:24])
        gram[p, place, :] = total
        gf = [net.send(gram.at[p, place], gram.at[p, place], peer) for peer in x_peers]

        def by_group(tiles):
            value = jnp.zeros((8, K), F32)
            for k, tile in enumerate(tiles):
                value = jnp.where(sub == k, tile, value)
            mean = group_mean(value, Z)
            return jnp.where(sub < Z, value - mean, 0.0), mean

        sz, mean_shift = by_group(tiles)
        weight = float(rows * 2 * X * Y)
        corr[0] = outer(sz, sz) * weight
        if first:
            for copy in yt:
                copy.wait_recv()
            means = [y_src[p, pl.ds(pl.multiple_of(24 + 8 * y, 8), 8)]]
            means += [sr_y[p, k, 24:32] for k in range(Y - 1)]
            means = jnp.concatenate(means, axis=0)
            group = group_mean(means, 8 * Y)
            m3c[...] = means - group
            m_src[...] = jnp.broadcast_to(group, (8, K))
            zt_flight = [net.send(m_src, m_in.at[k], peer) for k, peer in enumerate(z_peers)]
        else:
            corr[2] = outer(mzc[...], sz) * weight
        corr[1] = outer(m3c[...], shifts) * rows
        for copy in gf:
            copy.wait_recv()
        place = pl.ds(pl.multiple_of(c * (K // 2), K // 2), K // 2)
        last = net.send(gram.at[p, place], gram.at[p, place], core_peer)

        collect(0, (x, y), second_a, land2)
        collect(1, (y, x), second_b, land2)
        zsrc[:, : K // 2] = buf[0, x, y].T + corr[1, :, : K // 2]
        zsrc[:, K // 2 :] = buf[1, y, x].T + corr[1, :, K // 2 :]
        pf = [
            net.send(
                zsrc.at[pl.ds(pl.multiple_of(((z + k + 1) % Z) * share, share), share)],
                z_in.at[p, k],
                peer,
            )
            for k, peer in enumerate(z_peers)
        ]
        eye = lax.broadcasted_iota(jnp.int32, (K, K), 0) == lax.broadcasted_iota(jnp.int32, (K, K), 1)
        work[:, K:] = eye.astype(F32)
        last.wait_recv()
        work[:, :K] = gram[p] + corr[0]
        inverse_factor(work, fac)
        if first:
            for copy in zt_flight:
                copy.wait_recv()
            mzc[...], _ = by_group([m_src[...]] + [m_in[k] for k in range(Z - 1)])
            corr[2] = outer(mzc[...], sz) * weight
        place = pl.ds(pl.multiple_of(z * share, share), share)
        mine = zsrc[place, :] + corr[2, place, :]
        for k, copy in enumerate(pf):
            copy.wait_recv()
            mine = mine + z_in[p, k]
        net.drain()
        for j in range(X):
            for copy in panels(j):
                copy.wait_send()
        for j in range(X - 1):
            first_a(j).wait_send()
        for j in range(X):
            for k in range(1, Y):
                first_b(j, k).wait_send()
        return mine, shift - mean_shift

    mine, _ = reduce(0)
    panel = dot(mine, fac[...], ((1,), (1,)), HIGH).astype(BF16)
    place = pl.ds(pl.multiple_of(z * share, share), share)
    ph[x, c, y, place, :] = panel
    flight = [net.send(ph.at[x, c, y, place], ph.at[x, c, y, place], peer) for peer in z_peers]
    for copy in flight:
        copy.wait_recv()
    low, high = pl.ds(0, K // 2), pl.ds(K // 2, K // 2)
    near, far = ph.at[x, c, y, low], ph.at[x, c, y, high]
    flight_a = [net.send(near, near, y_peers[k - 1]) for k in (2, 1, 3)]
    flight_b = [net.send(far, far, x_peers[k - 1]) for k in (2, 1, 3)]
    for copy in flight_a:
        copy.wait_recv()
    last = []

    def forward(ref):
        last.append(net.send(ref, ref, core_peer))

    def slice_a(t):
        return ph.at[t, c, :, low]

    def slice_b(t):
        return ph.at[:, c, t, high]

    flight_a = {k: net.send(slice_a(x), slice_a(x), x_peers[k - 1]) for k in (2, 1, 3)}
    forward(slice_a(x))
    for copy in flight_b:
        copy.wait_recv()
    flight_b = {k: net.send(slice_b(y), slice_b(y), y_peers[k - 1]) for k in (2, 1, 3)}
    forward(slice_b(y))
    for k in (1, 3, 2):
        flight_a[k].wait_recv()
        forward(slice_a((x + RING - k) % RING))
        flight_b[k].wait_recv()
        forward(slice_b((y + RING - k) % RING))

    def second(core):
        def step(xx, carry):
            at = pl.multiple_of((xx * 2 + core) * Y * K, Y * K)
            right = ph[xx, core].reshape(Y * K, K)
            y_v[...] = y_v[...] + dot(e_v[:, pl.ds(at, Y * K)], right, ((1,), (0,)))
            return carry

        lax.fori_loop(0, X, step, 0)

    y_v[...] = jnp.zeros_like(y_v)
    second(c)
    for copy in last:
        copy.wait_recv()
    second(1 - c)
    net.drain()

    mine, offset = reduce(1)
    root = jnp.sqrt(jnp.full((1, K), rows * 2 * X * Y * Z, F32))
    basis[...] = dot(y_v[...] + offset, fac[...], ((1,), (1,)), HIGH) * root
    panel_t[...] = dot(mine, fac[...], ((1,), (1,)), HIGH) / root


def hand_on(basis_in, panel_in, basis_out, panel_out):
    basis_out[...] = basis_in[...]
    panel_out[...] = panel_in[...]


def on_device(dims, embeddings, sketch):
    X, Y, Z = dims
    rows, width = embeddings.shape
    share = K // Z
    record = 24 + 8 * Y
    vm = pltpu.VMEM
    transfers = 2 * (18 + 6 * (X + Y) + 3 * Z + X * Y) + Z + 4 * (X + Y)
    results = pl.pallas_call(
        functools.partial(kernel, dims),
        out_shape=(
            jax.ShapeDtypeStruct((rows, K), F32),
            jax.ShapeDtypeStruct((share, K), F32),
        ),
        in_specs=[pl.BlockSpec(memory_space=pl.ANY)] * 2,
        out_specs=(pl.BlockSpec(memory_space=vm), pl.BlockSpec(memory_space=vm)),
        scratch_shapes=[
            vm((rows, width), BF16),
            vm((width, K), BF16),
            vm((rows, K), F32),
            vm((2 * K + 16, rows), BF16),
            vm((rows, 2 * K), BF16),
            vm((2, RING, RING, K // 2, K), F32),
            vm((2, RING, RING, K // 2, K), F32),
            vm((2, 2, RING, RING, K // 2, K), F32),
            vm((2, 2, RING - 1, RING, K // 2, K), F32),
            vm((2, 2, RING - 1, K // 2, K), F32),
            vm((K, K), F32),
            vm((2, Z - 1, share, K), F32),
            vm((2, X, record, K), F32),
            vm((2, X, record, K), F32),
            vm((2, X - 1, record, K), F32),
            vm((2, record, K), F32),
            vm((2, Y - 1, 32, K), F32),
            vm((2, 24, K), F32),
            vm((2, Z - 1, 24, K), F32),
            vm((8 * Y, K), F32),
            vm((8, K), F32),
            vm((8, K), F32),
            vm((Z - 1, 8, K), F32),
            vm((3, K, K), F32),
            vm((2, K, K), F32),
            vm((K, 2 * K), F32),
            vm((K, K), F32),
            vm((X, 2, Y, K, K), BF16),
            pltpu.SemaphoreType.DMA((CHUNKS + 1,)),
            pltpu.SemaphoreType.DMA((transfers,)),
            pltpu.SemaphoreType.DMA((transfers,)),
        ],
        compiler_params=pltpu.CompilerParams(
            collective_id=0, has_side_effects=True, vmem_limit_bytes=56 * 1024 * 1024
        ),
        name="pca",
    )(embeddings, sketch)
    return pl.pallas_call(
        hand_on,
        out_shape=[jax.ShapeDtypeStruct(value.shape, F32) for value in results],
        in_specs=[pl.BlockSpec(memory_space=vm)] * 2,
        out_specs=[pl.BlockSpec(memory_space=vm)] * 2,
        name="hand_on",
    )(*results)


def solution(mesh):
    X, Y = mesh.shape["rowa"] // 2, 4
    dims = (X, Y, mesh.shape["rowb"] // Y)
    spread = P(("rowa", "rowb"), None)
    return jax.shard_map(
        functools.partial(on_device, dims),
        mesh=mesh,
        in_specs=(spread, P()),
        out_specs=(spread, spread),
        check_vma=False,
    )
```

```python
import functools

import jax
import jax.numpy as jnp
from jax import lax
from jax.experimental import pallas as pl
from jax.experimental.pallas import tpu as pltpu
from jax.sharding import PartitionSpec as P

F32 = jnp.float32
BF16 = jnp.bfloat16
HIGH = lax.Precision.HIGHEST
K = 128
RING = 4
CHUNKS = 4
BLOCK = 32


def dot(a, b, dims, precision=None):
    return lax.dot_general(a, b, (dims, ((), ())), precision=precision, preferred_element_type=F32)


def split(value):
    hi = value.astype(BF16)
    return hi, (value - hi.astype(F32)).astype(BF16)


class Net:
    def __init__(self, send_sem, recv_sem):
        self.send_sem, self.recv_sem = send_sem, recv_sem
        self.count = 0
        self.unsent = []

    def take(self, count):
        self.count += count
        return self.count - count

    def copy(self, slot, src, dst, device):
        return pltpu.make_async_remote_copy(
            src_ref=src,
            dst_ref=dst,
            send_sem=self.send_sem.at[slot],
            recv_sem=self.recv_sem.at[slot],
            device_id=device,
            device_id_type=pl.DeviceIdType.MESH,
        )

    def send(self, src, dst, device):
        copy = self.copy(self.take(1), src, dst, device)
        copy.start()
        self.unsent.append(copy)
        return copy

    def drain(self):
        for copy in self.unsent:
            copy.wait_send()
        self.unsent = []


def reciprocal(value):
    guess = pl.reciprocal(value, approx=True)
    return guess * (2.0 - value * guess)


def inverse_factor(work, out):
    sub = lax.broadcasted_iota(jnp.int32, (BLOCK, K), 0)
    count = K // BLOCK
    both = [work[i * BLOCK : (i + 1) * BLOCK, :] for i in range(count)]
    for b in range(count):
        gram, inv = both[b][:, :K], both[b][:, K:]
        at = b * BLOCK
        cols = [jnp.broadcast_to(gram[:, at + l : at + l + 1], (BLOCK, K)) for l in range(BLOCK)]
        pivots = jnp.ones((BLOCK, K), F32)
        for k in range(BLOCK):
            pivot = cols[k][k : k + 1, :]
            pivots = jnp.where(sub == k, pivot, pivots)
            mult = jnp.where(sub > k, cols[k] * reciprocal(pivot), 0.0)
            for l in range(k + 1, BLOCK):
                cols[l] = cols[l] - mult * cols[l][k : k + 1, :]
            gram = gram - mult * gram[k : k + 1, :]
            inv = inv - mult * inv[k : k + 1, :]
        scale = lax.rsqrt(pivots)
        scale = scale * (1.5 - 0.5 * pivots * scale * scale)
        gram = gram * scale
        inv = inv * scale
        out[at : at + BLOCK, :] = inv
        full = jnp.concatenate([gram, inv], axis=1)
        for start, stop in ((b + 1, b + 2), (b + 2, count)):
            if start < min(stop, count):
                left = gram[:, start * BLOCK : stop * BLOCK]
                update = dot(left, full, ((0,), (0,)), HIGH)
                for i in range(start, stop):
                    both[i] = both[i] - update[(i - start) * BLOCK : (i - start + 1) * BLOCK]


def kernel(
    dims, emb, sketch, basis, panel_t,
    e_v, om_v, y_v, zt, zc, buf, part, core_in, land1, land2, zsrc, z_in,
    sr, sr_core, sr_x, y_src, sr_y, z_rec, sr_z, m3c, mzc, m_src, m_in, corr, gram, work, fac, ph,
    load_sem, send_sem, recv_sem,
):
    X, Y, Z = dims
    rows = emb.shape[0]
    width = emb.shape[1]
    chunk = rows // CHUNKS
    share = K // Z

    def load(i):
        piece = pl.ds(pl.multiple_of(i * chunk, chunk), chunk)
        return pltpu.make_async_copy(emb.at[piece], e_v.at[piece], load_sem.at[i])

    load_sketch = pltpu.make_async_copy(sketch, om_v, load_sem.at[CHUNKS])
    load_sketch.start()
    for i in range(CHUNKS):
        load(i).start()

    a, b = lax.axis_index("rowa"), lax.axis_index("rowb")
    x, c = a // 2, a % 2
    y, z = b // Z, b % Z

    def dev(dx=0, dc=0, dy=0, dz=0):
        return (((x + dx) % X) * 2 + (c + dc) % 2, ((y + dy) % Y) * Z + (z + dz) % Z)

    core_peer = dev(dc=1)
    x_peers = [dev(dx=k) for k in range(1, X)]
    y_peers = [dev(dy=k) for k in range(1, Y)]
    z_peers = [dev(dz=k) for k in range(1, Z)]
    z_far = sorted(enumerate(z_peers), key=lambda kp: -min(kp[0] + 1, Z - 1 - kp[0]))
    peers = [core_peer] + x_peers + y_peers + z_peers
    barrier = pltpu.get_barrier_semaphore()
    for peer in peers:
        pl.semaphore_signal(barrier, inc=1, device_id=peer, device_id_type=pl.DeviceIdType.MESH)

    net = Net(send_sem, recv_sem)
    sub = lax.broadcasted_iota(jnp.int32, (8, K), 0)

    def group_mean(tile_rows, count):
        return jnp.sum(tile_rows, axis=0, keepdims=True) * (1.0 / count)

    def outer(left, right):
        return dot(left, right, ((0,), (0,)), HIGH)

    def sketch_chunk(i, carry):
        load(i).wait()
        piece = pl.ds(pl.multiple_of(i * chunk, chunk), chunk)
        y_v[piece, :] = dot(e_v[piece, :], om_v[...], ((1,), (0,)))
        return carry

    zt[2 * K :] = jnp.ones((16, rows), BF16)
    load_sketch.wait()
    lax.fori_loop(0, CHUNKS, sketch_chunk, 0)

    def center():
        first = jnp.sum(y_v[...], axis=0, keepdims=True) * (1.0 / rows)
        value = y_v[...] - first
        rest = jnp.sum(value, axis=0, keepdims=True) * (1.0 / rows)
        y_v[...] = value - rest
        return first + rest

    def products(core, xx, add, first):
        def step(half, carry):
            at = pl.multiple_of(((xx * 2 + core) * Y + 2 * half) * K, 2 * K)
            left = zt[...] if first else zt[: 2 * K]
            prod = dot(left, e_v[:, pl.ds(at, 2 * K)], ((1,), (0,)))
            sums = prod[2 * K : 2 * K + 1] * (1.0 / rows) if first else None
            prod = prod[:K] + prod[K : 2 * K]
            for k in range(2):
                yy = 2 * half + k
                if first:
                    tile = pl.ds(pl.multiple_of(24 + 8 * yy, 8), 8)
                    sr[core, xx, tile] = jnp.where(sub == a, sums[:, k * K : (k + 1) * K], 0.0)
                top = prod[: K // 2, k * K : (k + 1) * K]
                low = prod[K // 2 :, k * K : (k + 1) * K]
                if add is None:
                    part[0, xx, yy] = top
                    part[1, yy, xx] = low
                else:
                    buf[0, xx, yy] = top + core_in[add, 0, xx, yy]
                    buf[1, yy, xx] = low + core_in[add, 1, yy, xx]
            return carry

        lax.fori_loop(0, Y // 2, step, 0)

    def reduce(p):
        first = p == 0
        shift = center()
        hi, lo = split(y_v[...])
        zc[:, :K] = hi
        zc[:, K:] = lo
        zt[: 2 * K] = zc[...].T
        four = dot(zt[: 2 * K], zc[...], ((1,), (0,)))
        full = (four[:K, :K] + four[K:, K:]) + (four[:K, K:] + four[K:, :K])
        for cc in range(2):
            for xx in range(X):
                sr[cc, xx, 0:16] = full[(cc * X + xx) * 16 : (cc * X + xx + 1) * 16]
                sr[cc, xx, 16:24] = jnp.where(sub == a, shift, 0.0)
        if first:
            pl.semaphore_wait(barrier, len(peers))
        head, tail = pl.ds(0, 24), pl.ds(24, 8 * Y)
        flight = net.send(sr.at[1 - c, :, head], sr_core.at[p, :, head], core_peer)

        base = net.take(2 * X)

        def panels(j):
            xx = lax.rem(x + X - 1 - j, X)
            return [
                net.copy(base + 2 * j, part.at[0, xx], core_in.at[p, 0, xx], core_peer),
                net.copy(base + 2 * j + 1, part.at[1, :, xx], core_in.at[p, 1, :, xx], core_peer),
            ]

        def partner(j, carry):
            products(1 - c, lax.rem(x + X - 1 - j, X), None, first)
            for copy in panels(j):
                copy.start()
            return carry

        lax.fori_loop(0, 1, partner, 0)
        flight.wait_recv()
        sr[c, :, head] = sr[c, :, head] + sr_core[p, :, head]
        xf = [
            net.send(sr.at[c, (x + k + 1) % X, head], sr_x.at[p, k, head], peer)
            for k, peer in enumerate(x_peers)
        ]
        lax.fori_loop(1, X, partner, 0)
        if first:
            flight = net.send(sr.at[1 - c, :, tail], sr_core.at[p, :, tail], core_peer)

        base_a = net.take(X - 1)

        def first_a(j):
            k = X - 1 - j
            return net.copy(
                base_a + j, buf.at[0, lax.rem(x + k, X)], land1.at[p, 0, j], dev(dx=k)
            )

        base_b = net.take((Y - 1) * X)

        def first_b(j, k):
            xx = lax.rem(x + X - 1 - j, X)
            return net.copy(
                base_b + (Y - 1) * j + k - 1,
                buf.at[1, lax.rem(y + k, Y), xx],
                land1.at[p, 1, k - 1, xx],
                y_peers[k - 1],
            )

        def own(j, carry):
            for copy in panels(j):
                copy.wait_recv()
            products(c, lax.rem(x + X - 1 - j, X), p, first)

            @pl.when(j < X - 1)
            def _():
                first_a(j).start()

            @pl.when(j < X // 2)
            def _():
                for k in (2, 1, 3):
                    first_b(j, k).start()

            return carry

        lax.fori_loop(0, X, own, 0)

        record = sr[c, x, head]
        for copy in xf:
            copy.wait_recv()
        for k in range(X - 1):
            record = record + sr_x[p, k, head]
        y_src[p, head] = record
        yf = [
            net.send(y_src.at[p, head], sr_y.at[p, k, head], peer) for k, peer in enumerate(y_peers)
        ]
        for j in range(X // 2, X):
            for k in (2, 1, 3):
                first_b(j, k).start()
        if first:
            flight.wait_recv()
            sr[c, :, tail] = sr[c, :, tail] + sr_core[p, :, tail]
            xt = [
                net.send(sr.at[c, (x + k + 1) % X, tail], sr_x.at[p, k, tail], peer)
                for k, peer in enumerate(x_peers)
            ]
        for copy in yf:
            copy.wait_recv()
        own_gram = y_src[p, 0:16]
        shifts = [y_src[p, 16:24]]
        for k in range(Y - 1):
            own_gram = own_gram + sr_y[p, k, 0:16]
            shifts.append(sr_y[p, k, 16:24])
        shifts = jnp.concatenate(shifts, axis=0)
        group_shift = group_mean(shifts, 8 * Y)
        shifts = shifts - group_shift
        place = pl.ds(pl.multiple_of((c * X + x) * 16, 16), 16)
        corr[0] = outer(shifts, shifts) * rows
        z_rec[p, 0:16] = own_gram + corr[0, place, :]
        z_rec[p, 16:24] = jnp.broadcast_to(group_shift, (8, K))
        zf = [net.send(z_rec.at[p], sr_z.at[p, k], peer) for k, peer in z_far]

        def collect(g, at, copies, land):
            ref = buf.at[g, at[0]] if len(at) == 1 else buf.at[g, at[0], at[1]]
            total = ref[...]
            for copy in copies:
                copy.wait_recv()
            for k in range(RING - 1):
                total = total + land[p, g, k]
            ref[...] = total

        collect(0, (x,), [first_a(j) for j in range(X - 1)], land1)
        second_a = [
            net.send(buf.at[0, x, (y + k) % Y], land2.at[p, 0, k - 1], y_peers[k - 1]) for k in (2, 1, 3)
        ]
        if first:
            for copy in xt:
                copy.wait_recv()
            means = sr[c, x, tail]
            for k in range(X - 1):
                means = means + sr_x[p, k, tail]
            y_src[p, tail] = means
            yt = []
            for k, peer in enumerate(y_peers):
                tile = pl.ds(pl.multiple_of(24 + 8 * ((y + k + 1) % Y), 8), 8)
                yt.append(net.send(y_src.at[p, tile], sr_y.at[p, k, pl.ds(24, 8)], peer))
        collect(1, (y,), [first_b(j, k) for j in range(X) for k in range(1, Y)], land1)
        second_b = [
            net.send(buf.at[1, y, (x + k) % X], land2.at[p, 1, k - 1], x_peers[k - 1]) for k in (2, 1, 3)
        ]

        total = z_rec[p, 0:16]
        tiles = [z_rec[p, 16:24]]
        for copy in zf:
            copy.wait_recv()
        for k in range(Z - 1):
            total = total + sr_z[p, k, 0:16]
            tiles.append(sr_z[p, k, 16:24])
        gram[p, place, :] = total
        gf = [net.send(gram.at[p, place], gram.at[p, place], peer) for peer in x_peers]

        def by_group(tiles):
            value = jnp.zeros((8, K), F32)
            for k, tile in enumerate(tiles):
                value = jnp.where(sub == k, tile, value)
            mean = group_mean(value, Z)
            return jnp.where(sub < Z, value - mean, 0.0), mean

        sz, mean_shift = by_group(tiles)
        weight = float(rows * 2 * X * Y)
        corr[0] = outer(sz, sz) * weight
        if first:
            for copy in yt:
                copy.wait_recv()
            means = [y_src[p, pl.ds(pl.multiple_of(24 + 8 * y, 8), 8)]]
            means += [sr_y[p, k, 24:32] for k in range(Y - 1)]
            means = jnp.concatenate(means, axis=0)
            group = group_mean(means, 8 * Y)
            m3c[...] = means - group
            m_src[...] = jnp.broadcast_to(group, (8, K))
            zt_flight = [net.send(m_src, m_in.at[k], peer) for k, peer in z_far]
        else:
            corr[2] = outer(mzc[...], sz) * weight
        corr[1] = outer(m3c[...], shifts) * rows
        for copy in gf:
            copy.wait_recv()
        place = pl.ds(pl.multiple_of(c * (K // 2), K // 2), K // 2)
        last = net.send(gram.at[p, place], gram.at[p, place], core_peer)

        collect(0, (x, y), second_a, land2)
        collect(1, (y, x), second_b, land2)
        zsrc[:, : K // 2] = buf[0, x, y].T + corr[1, :, : K // 2]
        zsrc[:, K // 2 :] = buf[1, y, x].T + corr[1, :, K // 2 :]
        pf = [
            net.send(
                zsrc.at[pl.ds(pl.multiple_of(((z + k + 1) % Z) * share, share), share)],
                z_in.at[p, k],
                peer,
            )
            for k, peer in z_far
        ]
        eye = lax.broadcasted_iota(jnp.int32, (K, K), 0) == lax.broadcasted_iota(jnp.int32, (K, K), 1)
        work[:, K:] = eye.astype(F32)
        last.wait_recv()
        work[:, :K] = gram[p] + corr[0]
        inverse_factor(work, fac)
        if first:
            for copy in zt_flight:
                copy.wait_recv()
            mzc[...], _ = by_group([m_src[...]] + [m_in[k] for k in range(Z - 1)])
            corr[2] = outer(mzc[...], sz) * weight
        place = pl.ds(pl.multiple_of(z * share, share), share)
        mine = zsrc[place, :] + corr[2, place, :]
        for copy in pf:
            copy.wait_recv()
        for k in range(Z - 1):
            mine = mine + z_in[p, k]
        net.drain()
        for j in range(X):
            for copy in panels(j):
                copy.wait_send()
        for j in range(X - 1):
            first_a(j).wait_send()
        for j in range(X):
            for k in range(1, Y):
                first_b(j, k).wait_send()
        return mine, shift - mean_shift

    mine, _ = reduce(0)
    panel = dot(mine, fac[...], ((1,), (1,)), HIGH).astype(BF16)
    place = pl.ds(pl.multiple_of(z * share, share), share)
    ph[x, c, y, place, :] = panel
    flight = [net.send(ph.at[x, c, y, place], ph.at[x, c, y, place], peer) for _, peer in z_far]
    for copy in flight:
        copy.wait_recv()
    low, high = pl.ds(0, K // 2), pl.ds(K // 2, K // 2)
    near, far = ph.at[x, c, y, low], ph.at[x, c, y, high]
    flight_a = [net.send(near, near, y_peers[k - 1]) for k in (2, 1, 3)]
    flight_b = [net.send(far, far, x_peers[k - 1]) for k in (2, 1, 3)]
    for copy in flight_a:
        copy.wait_recv()
    near, far = ph.at[x, c, :, low], ph.at[:, c, y, high]
    flight_a = [net.send(near, near, x_peers[k - 1]) for k in (2, 1, 3)]
    for copy in flight_b:
        copy.wait_recv()
    flight_b = [net.send(far, far, y_peers[k - 1]) for k in (2, 1, 3)]
    for copy in flight_a:
        copy.wait_recv()
    near, far = ph.at[:, c, :, low], ph.at[:, c, :, high]
    last = [net.send(near, near, core_peer)]
    for copy in flight_b:
        copy.wait_recv()
    last.append(net.send(far, far, core_peer))

    def second(core):
        def step(xx, carry):
            at = pl.multiple_of((xx * 2 + core) * Y * K, Y * K)
            right = ph[xx, core].reshape(Y * K, K)
            y_v[...] = y_v[...] + dot(e_v[:, pl.ds(at, Y * K)], right, ((1,), (0,)))
            return carry

        lax.fori_loop(0, X, step, 0)

    y_v[...] = jnp.zeros_like(y_v)
    second(c)
    for copy in last:
        copy.wait_recv()
    second(1 - c)
    net.drain()

    mine, offset = reduce(1)
    root = jnp.sqrt(jnp.full((1, K), rows * 2 * X * Y * Z, F32))
    basis[...] = dot(y_v[...] + offset, fac[...], ((1,), (1,)), HIGH) * root
    panel_t[...] = dot(mine, fac[...], ((1,), (1,)), HIGH) / root


def hand_on(basis_in, panel_in, basis_out, panel_out):
    basis_out[...] = basis_in[...]
    panel_out[...] = panel_in[...]


def on_device(dims, embeddings, sketch):
    X, Y, Z = dims
    rows, width = embeddings.shape
    share = K // Z
    record = 24 + 8 * Y
    vm = pltpu.VMEM
    transfers = 2 * (18 + 6 * (X + Y) + 3 * Z + X * Y) + Z + 4 * (X + Y)
    results = pl.pallas_call(
        functools.partial(kernel, dims),
        out_shape=(
            jax.ShapeDtypeStruct((rows, K), F32),
            jax.ShapeDtypeStruct((share, K), F32),
        ),
        in_specs=[pl.BlockSpec(memory_space=pl.ANY)] * 2,
        out_specs=(pl.BlockSpec(memory_space=vm), pl.BlockSpec(memory_space=vm)),
        scratch_shapes=[
            vm((rows, width), BF16),
            vm((width, K), BF16),
            vm((rows, K), F32),
            vm((2 * K + 16, rows), BF16),
            vm((rows, 2 * K), BF16),
            vm((2, RING, RING, K // 2, K), F32),
            vm((2, RING, RING, K // 2, K), F32),
            vm((2, 2, RING, RING, K // 2, K), F32),
            vm((2, 2, RING - 1, RING, K // 2, K), F32),
            vm((2, 2, RING - 1, K // 2, K), F32),
            vm((K, K), F32),
            vm((2, Z - 1, share, K), F32),
            vm((2, X, record, K), F32),
            vm((2, X, record, K), F32),
            vm((2, X - 1, record, K), F32),
            vm((2, record, K), F32),
            vm((2, Y - 1, 32, K), F32),
            vm((2, 24, K), F32),
            vm((2, Z - 1, 24, K), F32),
            vm((8 * Y, K), F32),
            vm((8, K), F32),
            vm((8, K), F32),
            vm((Z - 1, 8, K), F32),
            vm((3, K, K), F32),
            vm((2, K, K), F32),
            vm((K, 2 * K), F32),
            vm((K, K), F32),
            vm((X, 2, Y, K, K), BF16),
            pltpu.SemaphoreType.DMA((CHUNKS + 1,)),
            pltpu.SemaphoreType.DMA((transfers,)),
            pltpu.SemaphoreType.DMA((transfers,)),
        ],
        compiler_params=pltpu.CompilerParams(
            collective_id=0, has_side_effects=True, vmem_limit_bytes=56 * 1024 * 1024
        ),
        name="pca",
    )(embeddings, sketch)
    return pl.pallas_call(
        hand_on,
        out_shape=[jax.ShapeDtypeStruct(value.shape, F32) for value in results],
        in_specs=[pl.BlockSpec(memory_space=vm)] * 2,
        out_specs=[pl.BlockSpec(memory_space=vm)] * 2,
        name="hand_on",
    )(*results)


def solution(mesh):
    X, Y = mesh.shape["rowa"] // 2, 4
    dims = (X, Y, mesh.shape["rowb"] // Y)
    spread = P(("rowa", "rowb"), None)
    return jax.shard_map(
        functools.partial(on_device, dims),
        mesh=mesh,
        in_specs=(spread, P()),
        out_specs=(spread, spread),
        check_vma=False,
    )
```

```python
import functools

import jax
import jax.numpy as jnp
from jax import lax
from jax.experimental import pallas as pl
from jax.experimental.pallas import tpu as pltpu
from jax.sharding import PartitionSpec as P

F32 = jnp.float32
BF16 = jnp.bfloat16
HIGH = lax.Precision.HIGHEST
K = 128
RING = 4
CHUNKS = 4
BLOCK = 32


def dot(a, b, dims, precision=None):
    return lax.dot_general(a, b, (dims, ((), ())), precision=precision, preferred_element_type=F32)


def split(value):
    hi = value.astype(BF16)
    return hi, (value - hi.astype(F32)).astype(BF16)


class Net:
    def __init__(self, send_sem, recv_sem):
        self.send_sem, self.recv_sem = send_sem, recv_sem
        self.count = 0
        self.unsent = []

    def take(self, count):
        self.count += count
        return self.count - count

    def copy(self, slot, src, dst, device):
        return pltpu.make_async_remote_copy(
            src_ref=src,
            dst_ref=dst,
            send_sem=self.send_sem.at[slot],
            recv_sem=self.recv_sem.at[slot],
            device_id=device,
            device_id_type=pl.DeviceIdType.MESH,
        )

    def send(self, src, dst, device):
        copy = self.copy(self.take(1), src, dst, device)
        copy.start()
        self.unsent.append(copy)
        return copy

    def drain(self):
        for copy in self.unsent:
            copy.wait_send()
        self.unsent = []


def reciprocal(value):
    guess = pl.reciprocal(value, approx=True)
    return guess * (2.0 - value * guess)


def inverse_factor(work, out):
    sub = lax.broadcasted_iota(jnp.int32, (BLOCK, K), 0)
    count = K // BLOCK
    both = [work[i * BLOCK : (i + 1) * BLOCK, :] for i in range(count)]
    for b in range(count):
        gram, inv = both[b][:, :K], both[b][:, K:]
        at = b * BLOCK
        cols = [jnp.broadcast_to(gram[:, at + l : at + l + 1], (BLOCK, K)) for l in range(BLOCK)]
        pivots = jnp.ones((BLOCK, K), F32)
        for k in range(BLOCK):
            pivot = cols[k][k : k + 1, :]
            pivots = jnp.where(sub == k, pivot, pivots)
            mult = jnp.where(sub > k, cols[k] * reciprocal(pivot), 0.0)
            for l in range(k + 1, BLOCK):
                cols[l] = cols[l] - mult * cols[l][k : k + 1, :]
            gram = gram - mult * gram[k : k + 1, :]
            inv = inv - mult * inv[k : k + 1, :]
        scale = lax.rsqrt(pivots)
        scale = scale * (1.5 - 0.5 * pivots * scale * scale)
        gram = gram * scale
        inv = inv * scale
        out[at : at + BLOCK, :] = inv
        full = jnp.concatenate([gram, inv], axis=1)
        for start, stop in ((b + 1, b + 2), (b + 2, count)):
            if start < min(stop, count):
                left = gram[:, start * BLOCK : stop * BLOCK]
                update = dot(left, full, ((0,), (0,)), HIGH)
                for i in range(start, stop):
                    both[i] = both[i] - update[(i - start) * BLOCK : (i - start + 1) * BLOCK]


def kernel(
    dims, emb, sketch, centred, factor, offset, panel_t,
    e_v, om_v, y_v, zt, zc, buf, part, core_in, land1, land2, zsrc, z_in,
    sr, sr_core, sr_x, y_src, sr_y, z_rec, sr_z, m3c, mzc, m_src, m_in, corr, gram, work, fac, ph,
    load_sem, store_sem, send_sem, recv_sem,
):
    X, Y, Z = dims
    rows = emb.shape[0]
    width = emb.shape[1]
    chunk = rows // CHUNKS
    share = K // Z

    def load(i):
        piece = pl.ds(pl.multiple_of(i * chunk, chunk), chunk)
        return pltpu.make_async_copy(emb.at[piece], e_v.at[piece], load_sem.at[i])

    load_sketch = pltpu.make_async_copy(sketch, om_v, load_sem.at[CHUNKS])
    load_sketch.start()
    for i in range(CHUNKS):
        load(i).start()

    a, b = lax.axis_index("rowa"), lax.axis_index("rowb")
    x, c = a // 2, a % 2
    y, z = b // Z, b % Z

    def dev(dx=0, dc=0, dy=0, dz=0):
        return (((x + dx) % X) * 2 + (c + dc) % 2, ((y + dy) % Y) * Z + (z + dz) % Z)

    core_peer = dev(dc=1)
    x_peers = [dev(dx=k) for k in range(1, X)]
    y_peers = [dev(dy=k) for k in range(1, Y)]
    z_peers = [dev(dz=k) for k in range(1, Z)]
    z_far = sorted(enumerate(z_peers), key=lambda kp: -min(kp[0] + 1, Z - 1 - kp[0]))
    peers = [core_peer] + x_peers + y_peers + z_peers
    barrier = pltpu.get_barrier_semaphore()
    for peer in peers:
        pl.semaphore_signal(barrier, inc=1, device_id=peer, device_id_type=pl.DeviceIdType.MESH)

    net = Net(send_sem, recv_sem)
    sub = lax.broadcasted_iota(jnp.int32, (8, K), 0)

    def group_mean(tile_rows, count):
        return jnp.sum(tile_rows, axis=0, keepdims=True) * (1.0 / count)

    def outer(left, right):
        return dot(left, right, ((0,), (0,)), HIGH)

    def sketch_chunk(i, carry):
        load(i).wait()
        piece = pl.ds(pl.multiple_of(i * chunk, chunk), chunk)
        y_v[piece, :] = dot(e_v[piece, :], om_v[...], ((1,), (0,)))
        return carry

    zt[2 * K :] = jnp.ones((16, rows), BF16)
    load_sketch.wait()
    lax.fori_loop(0, CHUNKS, sketch_chunk, 0)

    def center():
        first = jnp.sum(y_v[...], axis=0, keepdims=True) * (1.0 / rows)
        value = y_v[...] - first
        rest = jnp.sum(value, axis=0, keepdims=True) * (1.0 / rows)
        y_v[...] = value - rest
        return first + rest

    def products(core, xx, add, first):
        def step(half, carry):
            at = pl.multiple_of(((xx * 2 + core) * Y + 2 * half) * K, 2 * K)
            left = zt[...] if first else zt[: 2 * K]
            prod = dot(left, e_v[:, pl.ds(at, 2 * K)], ((1,), (0,)))
            sums = prod[2 * K : 2 * K + 1] * (1.0 / rows) if first else None
            prod = prod[:K] + prod[K : 2 * K]
            for k in range(2):
                yy = 2 * half + k
                if first:
                    tile = pl.ds(pl.multiple_of(24 + 8 * yy, 8), 8)
                    sr[core, xx, tile] = jnp.where(sub == a, sums[:, k * K : (k + 1) * K], 0.0)
                top = prod[: K // 2, k * K : (k + 1) * K]
                low = prod[K // 2 :, k * K : (k + 1) * K]
                if add is None:
                    part[0, xx, yy] = top
                    part[1, yy, xx] = low
                else:
                    buf[0, xx, yy] = top + core_in[add, 0, xx, yy]
                    buf[1, yy, xx] = low + core_in[add, 1, yy, xx]
            return carry

        lax.fori_loop(0, Y // 2, step, 0)

    store = pltpu.make_async_copy(y_v, centred, store_sem)

    def reduce(p):
        first = p == 0
        shift = center()
        if not first:
            store.start()
        hi, lo = split(y_v[...])
        zc[:, :K] = hi
        zc[:, K:] = lo
        zt[: 2 * K] = zc[...].T
        four = dot(zt[: 2 * K], zc[...], ((1,), (0,)))
        full = (four[:K, :K] + four[K:, K:]) + (four[:K, K:] + four[K:, :K])
        for cc in range(2):
            for xx in range(X):
                sr[cc, xx, 0:16] = full[(cc * X + xx) * 16 : (cc * X + xx + 1) * 16]
                sr[cc, xx, 16:24] = jnp.where(sub == a, shift, 0.0)
        if first:
            pl.semaphore_wait(barrier, len(peers))
        head, tail = pl.ds(0, 24), pl.ds(24, 8 * Y)
        flight = net.send(sr.at[1 - c, :, head], sr_core.at[p, :, head], core_peer)

        base = net.take(2 * X)

        def panels(j):
            xx = lax.rem(x + X - 1 - j, X)
            return [
                net.copy(base + 2 * j, part.at[0, xx], core_in.at[p, 0, xx], core_peer),
                net.copy(base + 2 * j + 1, part.at[1, :, xx], core_in.at[p, 1, :, xx], core_peer),
            ]

        def partner(j, carry):
            products(1 - c, lax.rem(x + X - 1 - j, X), None, first)
            for copy in panels(j):
                copy.start()
            return carry

        lax.fori_loop(0, 1, partner, 0)
        flight.wait_recv()
        sr[c, :, head] = sr[c, :, head] + sr_core[p, :, head]
        xf = [
            net.send(sr.at[c, (x + k + 1) % X, head], sr_x.at[p, k, head], peer)
            for k, peer in enumerate(x_peers)
        ]
        lax.fori_loop(1, X, partner, 0)
        if first:
            flight = net.send(sr.at[1 - c, :, tail], sr_core.at[p, :, tail], core_peer)

        base_a = net.take(X - 1)

        def first_a(j):
            k = X - 1 - j
            return net.copy(
                base_a + j, buf.at[0, lax.rem(x + k, X)], land1.at[p, 0, j], dev(dx=k)
            )

        base_b = net.take((Y - 1) * X)

        def first_b(j, k):
            xx = lax.rem(x + X - 1 - j, X)
            return net.copy(
                base_b + (Y - 1) * j + k - 1,
                buf.at[1, lax.rem(y + k, Y), xx],
                land1.at[p, 1, k - 1, xx],
                y_peers[k - 1],
            )

        def own(j, carry):
            for copy in panels(j):
                copy.wait_recv()
            products(c, lax.rem(x + X - 1 - j, X), p, first)

            @pl.when(j < X - 1)
            def _():
                first_a(j).start()

            @pl.when(j < X // 2)
            def _():
                for k in (2, 1, 3):
                    first_b(j, k).start()

            return carry

        lax.fori_loop(0, X, own, 0)

        record = sr[c, x, head]
        for copy in xf:
            copy.wait_recv()
        for k in range(X - 1):
            record = record + sr_x[p, k, head]
        y_src[p, head] = record
        yf = [
            net.send(y_src.at[p, head], sr_y.at[p, k, head], peer) for k, peer in enumerate(y_peers)
        ]
        for j in range(X // 2, X):
            for k in (2, 1, 3):
                first_b(j, k).start()
        if first:
            flight.wait_recv()
            sr[c, :, tail] = sr[c, :, tail] + sr_core[p, :, tail]
            xt = [
                net.send(sr.at[c, (x + k + 1) % X, tail], sr_x.at[p, k, tail], peer)
                for k, peer in enumerate(x_peers)
            ]
        for copy in yf:
            copy.wait_recv()
        own_gram = y_src[p, 0:16]
        shifts = [y_src[p, 16:24]]
        for k in range(Y - 1):
            own_gram = own_gram + sr_y[p, k, 0:16]
            shifts.append(sr_y[p, k, 16:24])
        shifts = jnp.concatenate(shifts, axis=0)
        group_shift = group_mean(shifts, 8 * Y)
        shifts = shifts - group_shift
        place = pl.ds(pl.multiple_of((c * X + x) * 16, 16), 16)
        corr[0] = outer(shifts, shifts) * rows
        z_rec[p, 0:16] = own_gram + corr[0, place, :]
        z_rec[p, 16:24] = jnp.broadcast_to(group_shift, (8, K))
        zf = [net.send(z_rec.at[p], sr_z.at[p, k], peer) for k, peer in z_far]

        def collect(g, at, copies, land):
            ref = buf.at[g, at[0]] if len(at) == 1 else buf.at[g, at[0], at[1]]
            total = ref[...]
            for copy in copies:
                copy.wait_recv()
            for k in range(RING - 1):
                total = total + land[p, g, k]
            ref[...] = total

        collect(0, (x,), [first_a(j) for j in range(X - 1)], land1)
        second_a = [
            net.send(buf.at[0, x, (y + k) % Y], land2.at[p, 0, k - 1], y_peers[k - 1]) for k in (2, 1, 3)
        ]
        if first:
            for copy in xt:
                copy.wait_recv()
            means = sr[c, x, tail]
            for k in range(X - 1):
                means = means + sr_x[p, k, tail]
            y_src[p, tail] = means
            yt = []
            for k, peer in enumerate(y_peers):
                tile = pl.ds(pl.multiple_of(24 + 8 * ((y + k + 1) % Y), 8), 8)
                yt.append(net.send(y_src.at[p, tile], sr_y.at[p, k, pl.ds(24, 8)], peer))
        collect(1, (y,), [first_b(j, k) for j in range(X) for k in range(1, Y)], land1)
        second_b = [
            net.send(buf.at[1, y, (x + k) % X], land2.at[p, 1, k - 1], x_peers[k - 1]) for k in (2, 1, 3)
        ]

        total = z_rec[p, 0:16]
        tiles = [z_rec[p, 16:24]]
        for copy in zf:
            copy.wait_recv()
        for k in range(Z - 1):
            total = total + sr_z[p, k, 0:16]
            tiles.append(sr_z[p, k, 16:24])
        gram[p, place, :] = total
        gf = [net.send(gram.at[p, place], gram.at[p, place], peer) for peer in x_peers]

        def by_group(tiles):
            value = jnp.zeros((8, K), F32)
            for k, tile in enumerate(tiles):
                value = jnp.where(sub == k, tile, value)
            mean = group_mean(value, Z)
            return jnp.where(sub < Z, value - mean, 0.0), mean

        sz, mean_shift = by_group(tiles)
        weight = float(rows * 2 * X * Y)
        corr[0] = outer(sz, sz) * weight
        if first:
            for copy in yt:
                copy.wait_recv()
            means = [y_src[p, pl.ds(pl.multiple_of(24 + 8 * y, 8), 8)]]
            means += [sr_y[p, k, 24:32] for k in range(Y - 1)]
            means = jnp.concatenate(means, axis=0)
            group = group_mean(means, 8 * Y)
            m3c[...] = means - group
            m_src[...] = jnp.broadcast_to(group, (8, K))
            zt_flight = [net.send(m_src, m_in.at[k], peer) for k, peer in z_far]
        else:
            corr[2] = outer(mzc[...], sz) * weight
        corr[1] = outer(m3c[...], shifts) * rows
        for copy in gf:
            copy.wait_recv()
        place = pl.ds(pl.multiple_of(c * (K // 2), K // 2), K // 2)
        last = net.send(gram.at[p, place], gram.at[p, place], core_peer)

        collect(0, (x, y), second_a, land2)
        collect(1, (y, x), second_b, land2)
        zsrc[:, : K // 2] = buf[0, x, y].T + corr[1, :, : K // 2]
        zsrc[:, K // 2 :] = buf[1, y, x].T + corr[1, :, K // 2 :]
        pf = [
            net.send(
                zsrc.at[pl.ds(pl.multiple_of(((z + k + 1) % Z) * share, share), share)],
                z_in.at[p, k],
                peer,
            )
            for k, peer in z_far
        ]
        eye = lax.broadcasted_iota(jnp.int32, (K, K), 0) == lax.broadcasted_iota(jnp.int32, (K, K), 1)
        work[:, K:] = eye.astype(F32)
        last.wait_recv()
        work[:, :K] = gram[p] + corr[0]
        inverse_factor(work, fac)
        if first:
            for copy in zt_flight:
                copy.wait_recv()
            mzc[...], _ = by_group([m_src[...]] + [m_in[k] for k in range(Z - 1)])
            corr[2] = outer(mzc[...], sz) * weight
        place = pl.ds(pl.multiple_of(z * share, share), share)
        mine = zsrc[place, :] + corr[2, place, :]
        for copy in pf:
            copy.wait_recv()
        for k in range(Z - 1):
            mine = mine + z_in[p, k]
        net.drain()
        for j in range(X):
            for copy in panels(j):
                copy.wait_send()
        for j in range(X - 1):
            first_a(j).wait_send()
        for j in range(X):
            for k in range(1, Y):
                first_b(j, k).wait_send()
        return mine, shift - mean_shift

    mine, _ = reduce(0)
    panel = dot(mine, fac[...], ((1,), (1,)), HIGH).astype(BF16)
    place = pl.ds(pl.multiple_of(z * share, share), share)
    ph[x, c, y, place, :] = panel
    flight = [net.send(ph.at[x, c, y, place], ph.at[x, c, y, place], peer) for _, peer in z_far]
    for copy in flight:
        copy.wait_recv()
    low, high = pl.ds(0, K // 2), pl.ds(K // 2, K // 2)
    near, far = ph.at[x, c, y, low], ph.at[x, c, y, high]
    flight_a = [net.send(near, near, y_peers[k - 1]) for k in (2, 1, 3)]
    flight_b = [net.send(far, far, x_peers[k - 1]) for k in (2, 1, 3)]
    for copy in flight_a:
        copy.wait_recv()
    near, far = ph.at[x, c, :, low], ph.at[:, c, y, high]
    flight_a = [net.send(near, near, x_peers[k - 1]) for k in (2, 1, 3)]
    for copy in flight_b:
        copy.wait_recv()
    flight_b = [net.send(far, far, y_peers[k - 1]) for k in (2, 1, 3)]
    for copy in flight_a:
        copy.wait_recv()
    near, far = ph.at[:, c, :, low], ph.at[:, c, :, high]
    last = [net.send(near, near, core_peer)]
    for copy in flight_b:
        copy.wait_recv()
    last.append(net.send(far, far, core_peer))

    def second(core):
        def step(xx, carry):
            at = pl.multiple_of((xx * 2 + core) * Y * K, Y * K)
            right = ph[xx, core].reshape(Y * K, K)
            y_v[...] = y_v[...] + dot(e_v[:, pl.ds(at, Y * K)], right, ((1,), (0,)))
            return carry

        lax.fori_loop(0, X, step, 0)

    y_v[...] = jnp.zeros_like(y_v)
    second(c)
    for copy in last:
        copy.wait_recv()
    second(1 - c)
    net.drain()

    mine, away = reduce(1)
    root = jnp.sqrt(jnp.full((1, K), rows * 2 * X * Y * Z, F32))
    panel_t[...] = dot(mine, fac[...], ((1,), (1,)), HIGH) / root
    factor[...] = fac[...] * root
    offset[...] = jnp.broadcast_to(away, (8, K))
    store.wait()


def hand_on(centred, factor, offset, panel_in, basis_out, panel_out):
    basis_out[...] = dot(centred[...] + offset[:1], factor[...], ((1,), (1,)), HIGH)
    panel_out[...] = panel_in[...]


def on_device(dims, embeddings, sketch):
    X, Y, Z = dims
    rows, width = embeddings.shape
    share = K // Z
    record = 24 + 8 * Y
    vm = pltpu.VMEM
    transfers = 2 * (18 + 6 * (X + Y) + 3 * Z + X * Y) + Z + 4 * (X + Y)
    results = pl.pallas_call(
        functools.partial(kernel, dims),
        out_shape=(
            jax.ShapeDtypeStruct((rows, K), F32),
            jax.ShapeDtypeStruct((K, K), F32),
            jax.ShapeDtypeStruct((8, K), F32),
            jax.ShapeDtypeStruct((share, K), F32),
        ),
        in_specs=[pl.BlockSpec(memory_space=pl.ANY)] * 2,
        out_specs=(pl.BlockSpec(memory_space=pl.ANY),) + (pl.BlockSpec(memory_space=vm),) * 3,
        scratch_shapes=[
            vm((rows, width), BF16),
            vm((width, K), BF16),
            vm((rows, K), F32),
            vm((2 * K + 16, rows), BF16),
            vm((rows, 2 * K), BF16),
            vm((2, RING, RING, K // 2, K), F32),
            vm((2, RING, RING, K // 2, K), F32),
            vm((2, 2, RING, RING, K // 2, K), F32),
            vm((2, 2, RING - 1, RING, K // 2, K), F32),
            vm((2, 2, RING - 1, K // 2, K), F32),
            vm((K, K), F32),
            vm((2, Z - 1, share, K), F32),
            vm((2, X, record, K), F32),
            vm((2, X, record, K), F32),
            vm((2, X - 1, record, K), F32),
            vm((2, record, K), F32),
            vm((2, Y - 1, 32, K), F32),
            vm((2, 24, K), F32),
            vm((2, Z - 1, 24, K), F32),
            vm((8 * Y, K), F32),
            vm((8, K), F32),
            vm((8, K), F32),
            vm((Z - 1, 8, K), F32),
            vm((3, K, K), F32),
            vm((2, K, K), F32),
            vm((K, 2 * K), F32),
            vm((K, K), F32),
            vm((X, 2, Y, K, K), BF16),
            pltpu.SemaphoreType.DMA((CHUNKS + 1,)),
            pltpu.SemaphoreType.DMA,
            pltpu.SemaphoreType.DMA((transfers,)),
            pltpu.SemaphoreType.DMA((transfers,)),
        ],
        compiler_params=pltpu.CompilerParams(
            collective_id=0, has_side_effects=True, vmem_limit_bytes=56 * 1024 * 1024
        ),
        name="pca",
    )(embeddings, sketch)
    return pl.pallas_call(
        hand_on,
        out_shape=[jax.ShapeDtypeStruct(results[k].shape, F32) for k in (0, 3)],
        in_specs=[pl.BlockSpec(memory_space=vm)] * 4,
        out_specs=[pl.BlockSpec(memory_space=vm)] * 2,
        name="hand_on",
    )(*results)


def solution(mesh):
    X, Y = mesh.shape["rowa"] // 2, 4
    dims = (X, Y, mesh.shape["rowb"] // Y)
    spread = P(("rowa", "rowb"), None)
    return jax.shard_map(
        functools.partial(on_device, dims),
        mesh=mesh,
        in_specs=(spread, P()),
        out_specs=(spread, spread),
        check_vma=False,
    )
```
